256 devices in a mesh: src: 32 (over y_hi, z, core), tgt: 8 (over y_lo, x).
Axes of the slice: x: 4, y: 4 (y_hi: 2, y_lo: 2; y = y_hi * 2 + y_lo), z: 8, core: 2. Of those that a mesh axis runs over, the one named last changes fastest.
Arguments:
- source_cells: float32 [32, 32768], P(None, 'src'), may hold values from -2.6 to 2.6
- target_cells: float32 [32, 32768], P(None, 'tgt'), may hold values from -0.6 to 0.6
- start_potential: float32 [32768], P('tgt'), may hold values from -0.3 to 0.3
Outputs:
- source_potential: float32 [32768], P('src')
- target_potential: float32 [32768], P('tgt')
- source_image: float32 [32, 32768], P(None, 'src')
- target_image: float32 [32, 32768], P(None, 'tgt')
The draws below stay inside these ranges and needn't reach their ends.
All inputs are finite; a program needn't handle non-finite values.
Results may differ from the reference program's by a relative error of at most 0.0003.
Values sent between devices are 32-bit elements; how exact they have to be, the bound alone decides.
No kernel may reach another device: no remote copies, remote signals or barrier semaphores. Data moves between devices by JAX's collectives and lax.ppermute only.
A program may use at most 64 MiB of HBM per device.

```python
import math
import jax
import jax.numpy as jnp
from jax import lax

K = 32
NS = 32768
NT = 32768


def draw_source_cells(key, part):
    key = jax.random.fold_in(key, 11)
    base_key = jax.random.fold_in(key, 0)
    cells = 0.1 * jax.random.truncated_normal(base_key, -4.0, 4.0, (K, NS), jnp.float32)
    return cells


def level_of(own_key, shape, shards, smallest, high):
    def one(position, parts):
        steps = jax.random.uniform(jax.random.fold_in(jax.random.fold_in(own_key, 6), position), (parts,), jnp.float32, smallest / len(shards), high / len(shards))
        return jnp.repeat(jnp.exp(steps), shape[position] // parts).reshape((-1,) + (1,) * (len(shape) - position - 1))

    loudness = one(*shards[0])
    for cut in shards[1:]:
        loudness = loudness * one(*cut)
    return loudness


def centred(key, dims, scale, reach, cuts=(), kind=jnp.bfloat16):
    result = scale * jax.random.normal(key, dims, jnp.float32)
    if cuts:
        result = result * level_of(key, dims, cuts, -0.22, 0.18)
    return jnp.clip(result, -reach, reach).astype(kind)


def setup_inputs(seed: int = 0) -> dict:
    splits = jax.random.split(jax.random.key(seed), 4)
    source_cells = draw_source_cells(jax.random.fold_in(splits[3], 71), 0)
    target_cells = centred(splits[1], (K, NT), 0.1, 0.6, ((1, 8),), jnp.float32)
    start_potential = centred(splits[2], (NT,), 0.05, 0.3, ((0, 8),), jnp.float32)
    return {"source_cells": source_cells, "target_cells": target_cells, "start_potential": start_potential}


EPS = 0.05


def cross_cost(left, right):
    cross = lax.dot_general(left, right, (((0,), (0,)), ((), ())), precision=lax.Precision.HIGHEST, preferred_element_type=jnp.float32)
    return jnp.sum(left * left, 0)[:, None] + jnp.sum(right * right, 0)[None, :] - 2.0 * cross


def log_total(scores, axis):
    peak = jnp.max(scores, axis, keepdims=True)
    return jnp.squeeze(peak, axis) + jnp.log(jnp.sum(jnp.exp(scores - peak), axis))


def reference(source_cells, target_cells, start_potential):
    src_block = math.gcd(512, NS)
    tgt_block = math.gcd(512, NT)
    src_parts = source_cells.reshape(K, NS // src_block, src_block).transpose(1, 0, 2)
    tgt_parts = target_cells.reshape(K, NT // tgt_block, tgt_block).transpose(1, 0, 2)

    def row_step(block):
        cost = cross_cost(block, target_cells)
        return log_total((start_potential[None, :] - cost) / EPS, 1)

    row_lse = lax.map(row_step, src_parts).reshape(NS)
    source_potential = -EPS * jnp.log(jnp.float32(NS)) - EPS * row_lse

    def column_step(block):
        cost = cross_cost(source_cells, block)
        return log_total((source_potential[:, None] - cost) / EPS, 0)

    column_lse = lax.map(column_step, tgt_parts).reshape(NT)
    target_potential = -EPS * jnp.log(jnp.float32(NT)) - EPS * column_lse
    src_pots = source_potential.reshape(NS // src_block, src_block)
    tgt_pots = target_potential.reshape(NT // tgt_block, tgt_block)

    def source_step(pair):
        block, pots = pair
        plan = jnp.exp((pots[:, None] + target_potential[None, :] - cross_cost(block, target_cells)) / EPS)
        numer = lax.dot_general(target_cells, plan, (((1,), (1,)), ((), ())), precision=lax.Precision.HIGHEST, preferred_element_type=jnp.float32)
        return numer / jnp.sum(plan, 1)[None, :]

    def target_step(pair):
        block, pots = pair
        plan = jnp.exp((source_potential[:, None] + pots[None, :] - cross_cost(source_cells, block)) / EPS)
        numer = jnp.dot(source_cells, plan, precision=lax.Precision.HIGHEST, preferred_element_type=jnp.float32)
        return numer / jnp.sum(plan, 0)[None, :]

    source_image = lax.map(source_step, (src_parts, src_pots)).transpose(1, 0, 2).reshape(K, NS)
    target_image = lax.map(target_step, (tgt_parts, tgt_pots)).transpose(1, 0, 2).reshape(K, NT)
    return source_potential, target_potential, source_image, target_image
```

```python
import functools
import math

import jax
import jax.numpy as jnp
from jax import lax
from jax.experimental import pallas as pl
from jax.experimental.pallas import tpu as pltpu
from jax.sharding import PartitionSpec as P

EPS = 0.05
C2 = 1.4426950408889634 / EPS
LN = EPS * math.log(2.0)
BF = jnp.bfloat16
F32 = jnp.float32
K = 32
KD = 8 * K
VM = pl.BlockSpec(memory_space=pltpu.VMEM)
SM = pl.BlockSpec(memory_space=pltpu.SMEM)
LANES = 128


def thirds(v):
    hi = v.astype(BF)
    rest = v - hi.astype(F32)
    mid = rest.astype(BF)
    return hi, mid, (rest - mid.astype(F32)).astype(BF)


def left_rows(v):
    hi, mid, lo = thirds(v)
    return jnp.concatenate([hi, hi, hi, mid, mid, lo], 0)


def right_rows(v):
    hi, mid, lo = thirds(v)
    return jnp.concatenate([hi, mid, lo, hi, mid, hi], 0)


def bias_rows(b):
    hi, mid, lo = (part.astype(F32) for part in thirds(b))
    row = lax.broadcasted_iota(jnp.int32, (2 * K, b.shape[1]), 0)
    return jnp.where(row == 0, hi, jnp.where(row == 1, mid, jnp.where(row == 2, lo, 0.0))).astype(BF)


def halves(v):
    hi = v.astype(BF)
    return hi, (v - hi.astype(F32)).astype(BF)


def merge(logs, images):
    top = functools.reduce(jnp.maximum, logs)
    shares = [jnp.exp2(one - top) for one in logs]
    mass = functools.reduce(jnp.add, shares)
    image = functools.reduce(jnp.add, [w * i for w, i in zip(shares, images)])
    return top + jnp.log2(mass), image / mass


def row_sums(x_ref, y_ref, g_ref, out_ref, a_ref, b_ref, t_ref, m_ref, s_ref):
    ns, nt = x_ref.shape[1], y_ref.shape[1]
    rows_at_once = t_ref.shape[0]
    a_ref[...] = jnp.concatenate([left_rows(x_ref[...] * (2 * C2)), jnp.ones((2 * K, ns), BF)], 0).T
    y = y_ref[...]
    b_ref[0 : 6 * K, :] = right_rows(y)
    b_ref[6 * K : KD, :] = bias_rows((g_ref[...] - jnp.sum(y * y, 0, keepdims=True)) * C2)

    def block(r, _):
        rows = pl.ds(pl.multiple_of(r * rows_at_once, rows_at_once), rows_at_once)
        t_ref[...] = jnp.dot(a_ref[rows, :], b_ref[...], preferred_element_type=F32)
        cuts = [slice(c, c + LANES) for c in range(0, nt, LANES)]
        peak = functools.reduce(jnp.maximum, [t_ref[:, cut] for cut in cuts])
        m_ref[rows, :] = peak
        s_ref[rows, :] = functools.reduce(jnp.add, [jnp.exp2(t_ref[:, cut] - peak) for cut in cuts])
        return 0

    lax.fori_loop(0, ns // rows_at_once, block, 0)
    peak = m_ref[...].T
    top = jnp.max(peak, 0, keepdims=True)
    total = top + jnp.log2(jnp.sum(s_ref[...].T * jnp.exp2(peak - top), 0, keepdims=True))
    for d in range(out_ref.shape[0]):
        for k in range(ns // LANES):
            out_ref[d, k : k + 1, :] = total[:, k * LANES : (k + 1) * LANES]


def column_sums(log_n, core_ref, x_ref, y_ref, part_ref, pot_ref, keep_ref, send_ref, a_ref, b_ref, v_ref, t_ref):
    ns, nt = x_ref.shape[1], y_ref.shape[1]
    width = t_ref.shape[1]
    parts = part_ref[...]
    top = jnp.max(parts, 0)
    total = top + jnp.log2(jnp.sum(jnp.exp2(parts - top[None]), 0))
    total = jnp.concatenate([total[k : k + 1, :] for k in range(ns // LANES)], 1) + log_n
    x = x_ref[...]
    pot_ref[...] = jnp.sum(x * x, 0, keepdims=True) - LN * total
    a_ref[...] = jnp.concatenate([left_rows(x * (2 * C2)), bias_rows(-total)], 0).T
    b_ref[0 : 6 * K, :] = right_rows(y_ref[...])
    b_ref[6 * K : KD, :] = jnp.ones((2 * K, nt), BF)
    hi, lo = halves(x)
    v_ref[...] = jnp.concatenate([hi, lo, jnp.ones((K // 2, ns), BF)], 0)

    def work(out_ref, start, chunk):
        cols = pl.ds(pl.multiple_of(start + chunk * width, width), width)
        t_ref[...] = jnp.dot(a_ref[...], b_ref[:, cols], preferred_element_type=F32)
        peak = jnp.max(t_ref[...], 0, keepdims=True)
        hi, lo = halves(jnp.exp2(t_ref[...] - peak))
        sums = jnp.dot(v_ref[...], hi, preferred_element_type=F32) + jnp.dot(v_ref[...], lo, preferred_element_type=F32)
        mass = sums[2 * K : 2 * K + 1, :]
        image = (sums[0:K, :] + sums[K : 2 * K, :]) / mass
        logs = jnp.broadcast_to(peak + jnp.log2(mass), (8, width))
        per = width // LANES
        for k in range(per):
            out_ref[chunk * per + k, 0:K, :] = image[:, k * LANES : (k + 1) * LANES]
            out_ref[chunk * per + k, K : K + 8, :] = logs[:, k * LANES : (k + 1) * LANES]
        return 0

    core = core_ref[0]
    half = nt // 2
    lax.fori_loop(0, half // width, lambda c, _: work(send_ref, (1 - core) * half, c), 0)
    lax.fori_loop(0, half // width, lambda c, _: work(keep_ref, core * half, c), 0)


def merge_pair(one_ref, two_ref, out_ref):
    log, image = merge(
        [one_ref[:, K : K + 8, :][:, 0:1, :], two_ref[:, K : K + 8, :][:, 0:1, :]],
        [one_ref[:, 0:K, :], two_ref[:, 0:K, :]],
    )
    out_ref[:, 0:K, :] = image
    out_ref[:, K : K + 8, :] = jnp.broadcast_to(log, (out_ref.shape[0], 8, LANES))


def merge_chunk(part_ref, out_ref):
    n = part_ref.shape[0]
    log, image = merge([part_ref[d, K : K + 1, :] for d in range(n)], [part_ref[d, 0:K, :] for d in range(n)])
    for d in range(n):
        out_ref[d, 0:K, :] = image
        out_ref[d, K : K + 8, :] = jnp.broadcast_to(log, (8, LANES))


def row_images(
    log_n, core_ref, x_ref, y_ref, mine_ref, other_ref, pot_ref, img_ref, out_ref, a_ref, b_ref, v_ref, t_ref, o_ref, l_ref
):
    ns, nt = x_ref.shape[1], y_ref.shape[1]
    rows_at_once = t_ref.shape[0]
    core = core_ref[0]
    for side, ref in ((core, mine_ref), (1 - core, other_ref)):
        for q in range(ref.shape[0]):
            cols = pl.ds(pl.multiple_of(side * (nt // 2) + q * LANES, LANES), LANES)
            img_ref[:, cols] = ref[q, 0:K, :]
            l_ref[:, cols] = ref[q, K : K + 8, :]
    total = l_ref[0:1, :] + log_n
    y = y_ref[...]
    pot_ref[...] = jnp.sum(y * y, 0, keepdims=True) - LN * total
    a_ref[...] = jnp.concatenate([left_rows(x_ref[...] * (2 * C2)), jnp.ones((2 * K, ns), BF)], 0).T
    b_ref[0 : 6 * K, :] = right_rows(y)
    b_ref[6 * K : KD, :] = bias_rows(-total)
    hi, lo = halves(y)
    v_ref[...] = jnp.concatenate([hi, lo, jnp.ones((2 * K, nt), BF)], 0)
    by_last = (((1,), (1,)), ((), ()))

    def block(r, _):
        rows = pl.ds(pl.multiple_of(r * rows_at_once, rows_at_once), rows_at_once)
        t_ref[...] = jnp.dot(a_ref[rows, :], b_ref[...], preferred_element_type=F32)
        peak = functools.reduce(jnp.maximum, [t_ref[:, c : c + LANES] for c in range(0, nt, LANES)])
        peak = jnp.max(peak, 1, keepdims=True)
        hi, lo = halves(jnp.exp2(t_ref[...] - peak))
        sums = lax.dot_general(hi, v_ref[...], by_last, preferred_element_type=F32)
        sums += lax.dot_general(lo, v_ref[...], by_last, preferred_element_type=F32)
        mass = sums[:, 2 * K : 2 * K + 1]
        lane = lax.broadcasted_iota(jnp.int32, sums.shape, 1)
        o_ref[rows, :] = jnp.where(lane < 2 * K, sums / mass, peak + jnp.log2(mass))
        return 0

    lax.fori_loop(0, ns // rows_at_once, block, 0)
    sums = o_ref[...].T
    image = sums[0:K, :] + sums[K : 2 * K, :]
    tiles = ns // LANES
    for d in range(out_ref.shape[0]):
        for k in range(tiles):
            cut = slice(k * LANES, (k + 1) * LANES)
            out_ref[d, 0, k : k + 1, :] = sums[2 * K : 2 * K + 1, cut]
            for r in range(K // 8):
                out_ref[d, 1 + r * tiles + k] = image[8 * r : 8 * r + 8, cut]


def merge_rows(part_ref, out_ref):
    n, tiles = part_ref.shape[0], out_ref.shape[1] // LANES
    logs = [part_ref[d, 0] for d in range(n)]
    top = functools.reduce(jnp.maximum, logs)
    shares = [jnp.exp2(one - top) for one in logs]
    mass = functools.reduce(jnp.add, shares)
    shares = [one / mass for one in shares]
    for k in range(tiles):
        weights = [jnp.broadcast_to(one[k : k + 1, :], (8, LANES)) for one in shares]
        for r in range(K // 8):
            image = functools.reduce(jnp.add, [weights[d] * part_ref[d, 1 + r * tiles + k] for d in range(n)])
            out_ref[8 * r : 8 * r + 8, k * LANES : (k + 1) * LANES] = image


def call(kernel, ins, outs, scratch=()):
    return pl.pallas_call(
        kernel,
        out_shape=tuple(jax.ShapeDtypeStruct(shape, F32) for shape in outs),
        in_specs=[SM if spec == "s" else VM for spec in ins],
        out_specs=tuple(VM for _ in outs),
        scratch_shapes=[pltpu.VMEM(shape, dtype) for shape, dtype in scratch],
        compiler_params=pltpu.CompilerParams(vmem_limit_bytes=50 << 20),
    )


def solution(mesh):
    n_src, n_tgt = mesh.shape["src"], mesh.shape["tgt"]
    pairs = n_src // 2
    across = [[c + 2 * q for q in range(pairs)] for c in range(2)]
    swap = [(i, i ^ 1) for i in range(n_src)]

    def shards(x, y, g):
        ns, nt = x.shape[1], y.shape[1]
        tiles = ns // LANES
        core = (lax.axis_index("src") % 2).astype(jnp.int32).reshape(1)
        operands = [((ns, KD), BF), ((KD, nt), BF)]
        chunk = (pairs, K + 8, LANES)

        (part,) = call(
            row_sums,
            "vvv",
            [(n_tgt, tiles, LANES)],
            operands + [((256, nt), F32), ((ns, LANES), F32), ((ns, LANES), F32)],
        )(x, y, g.reshape(1, nt))
        part = lax.all_to_all(part, "tgt", 0, 0, tiled=True)

        source_potential, keep, send = call(
            functools.partial(column_sums, math.log2(ns * n_src)),
            "svvv",
            [(1, ns), chunk, chunk],
            operands + [((80, ns), BF), ((ns, 1024), F32)],
        )(core, x, y, part)
        (merged,) = call(merge_pair, "vv", [chunk])(keep, lax.ppermute(send, "src", swap))
        merged = lax.all_to_all(merged, "src", 0, 0, axis_index_groups=across, tiled=True)
        (whole,) = call(merge_chunk, "v", [chunk])(merged)
        mine = lax.all_to_all(whole, "src", 0, 0, axis_index_groups=across, tiled=True)
        other = lax.ppermute(mine, "src", swap)

        target_potential, target_image, part = call(
            functools.partial(row_images, math.log2(nt * n_tgt)),
            "svvvv",
            [(1, nt), (K, nt), (n_tgt, 1 + K // 8 * tiles, 8, LANES)],
            operands + [((LANES, nt), BF), ((256, nt), F32), ((ns, LANES), F32), ((8, nt), F32)],
        )(core, x, y, mine, other)
        part = lax.all_to_all(part, "tgt", 0, 0, tiled=True)
        (source_image,) = call(merge_rows, "v", [(K, ns)])(part)
        return source_potential.reshape(ns), target_potential.reshape(nt), source_image, target_image

    return jax.shard_map(
        shards,
        mesh=mesh,
        in_specs=(P(None, "src"), P(None, "tgt"), P("tgt")),
        out_specs=(P("src"), P("tgt"), P(None, "src"), P(None, "tgt")),
        check_vma=False,
    )
```

```python
import functools
import math

import jax
import jax.numpy as jnp
from jax import lax
from jax.experimental import pallas as pl
from jax.experimental.pallas import tpu as pltpu
from jax.sharding import PartitionSpec as P

EPS = 0.05
C2 = 1.4426950408889634 / EPS
LN = EPS * math.log(2.0)
LEAST = 2.0**-80
LIFT = 64.0
BF = jnp.bfloat16
F32 = jnp.float32
K = 32
KD = 8 * K
VM = pl.BlockSpec(memory_space=pltpu.VMEM)
SM = pl.BlockSpec(memory_space=pltpu.SMEM)
LANES = 128
TALL, WIDE = 1024, 512
BLOCK = ((TALL, WIDE), F32)


def thirds(v):
    hi = v.astype(BF)
    rest = v - hi.astype(F32)
    mid = rest.astype(BF)
    return hi, mid, (rest - mid.astype(F32)).astype(BF)


def halves(v):
    hi = v.astype(BF)
    return hi, (v - hi.astype(F32)).astype(BF)


def offsets(b, first):
    hi, mid, lo = (part.astype(F32) for part in thirds(b))
    row = lax.broadcasted_iota(jnp.int32, (2 * K, b.shape[1]), 0)
    row, one = (row, row - 3) if first else (row - 3, row)
    value = jnp.where(row == 0, hi, jnp.where(row == 1, mid, jnp.where(row == 2, lo, 0.0)))
    return jnp.where((one >= 0) & (one < 3), 1.0, value).astype(BF)


def first_side(v, b):
    hi, mid, lo = thirds(v)
    return jnp.concatenate([hi, hi, hi, mid, mid, lo, offsets(b, True)], 0)


def second_side(v, b):
    hi, mid, lo = thirds(v)
    return jnp.concatenate([hi, mid, lo, hi, mid, hi, offsets(b, False)], 0)


def coordinates(v):
    hi, lo = halves(v)
    return jnp.concatenate([hi, lo, jnp.ones((K // 2, v.shape[1]), BF)], 0)


def cut(tiles, k):
    return tiles[:, k * LANES : (k + 1) * LANES]


def blocks(a_ref, b_ref, t_refs, first, use):
    tall, wide = t_refs[0].shape
    places = [(r, c) for c in range(first, first + b_ref.shape[1], wide) for r in range(0, a_ref.shape[0], tall)]

    def fill(i):
        r, c = places[i]
        t_refs[i % 2][...] = jnp.dot(a_ref[r : r + tall, :], b_ref[:, c : c + wide], preferred_element_type=F32)

    fill(0)
    for i, (r, c) in enumerate(places):
        if i + 1 < len(places):
            fill(i + 1)
        use(t_refs[i % 2], slice(r, r + tall), slice(c, c + wide))


def log_sums(a_ref, b_ref, t_refs, l_ref):
    tall, wide = t_refs[0].shape

    def use(t_ref, rows, cols):
        part = jnp.sum(jnp.exp2(t_ref[...]), 0, keepdims=True)
        l_ref[:, cols] = part if rows.start == 0 else l_ref[:, cols] + part

    blocks(a_ref, b_ref, t_refs, 0, use)
    least = jnp.min(l_ref[...])
    l_ref[...] = jnp.log2(l_ref[...])

    @pl.when(least < LEAST)
    def _():
        t_ref = t_refs[0]

        def column(c, _):
            cols = pl.ds(pl.multiple_of(c * wide, wide), wide)

            def fill(r):
                rows = pl.ds(pl.multiple_of(r * tall, tall), tall)
                t_ref[...] = jnp.dot(a_ref[rows, :], b_ref[:, cols], preferred_element_type=F32)

            def highest(r, peak):
                fill(r)
                return jnp.maximum(peak, jnp.max(t_ref[...], 0, keepdims=True))

            count = a_ref.shape[0] // tall
            peak = lax.fori_loop(0, count, highest, jnp.full((1, wide), -1e30, F32))

            def add(r, total):
                fill(r)
                return total + jnp.sum(jnp.exp2(t_ref[...] - peak), 0, keepdims=True)

            l_ref[:, cols] = peak + jnp.log2(lax.fori_loop(0, count, add, jnp.zeros((1, wide), F32)))
            return 0

        lax.fori_loop(0, b_ref.shape[1] // wide, column, 0)


def weighted(a_ref, b_ref, v_ref, t_refs, o_ref):
    def use(t_ref, rows, cols):
        hi, lo = halves(jnp.exp2(t_ref[...]))
        part = jnp.dot(v_ref[:, rows], hi, preferred_element_type=F32)
        part += jnp.dot(v_ref[:, rows], lo, preferred_element_type=F32)
        o_ref[:, cols] = part if rows.start == 0 else o_ref[:, cols] + part

    blocks(a_ref, b_ref, t_refs, 0, use)


def row_logs(x_ref, y_ref, g_ref, out_ref, a_ref, b_ref, l_ref, *t_refs):
    x, y = x_ref[...], y_ref[...]
    y_sq = jnp.sum(y * y, 0, keepdims=True)
    lift = (g_ref[...] - y_sq) * C2
    longest = jnp.sqrt(jnp.sum(x * x, 0, keepdims=True)) * jnp.sqrt(jnp.max(y_sq, 1, keepdims=True))
    bound = jnp.max(lift, 1, keepdims=True) + 2 * C2 * longest
    a_ref[...] = first_side(y, lift).T
    b_ref[...] = second_side(x * (2 * C2), -bound)
    log_sums(a_ref, b_ref, t_refs, l_ref)
    total = l_ref[...] + bound
    for k in range(out_ref.shape[1]):
        for d in range(out_ref.shape[0]):
            out_ref[d, k : k + 1, :] = cut(total, k)


def column_logs(log_n, x_ref, y_ref, g_ref, part_ref, pot_ref, total_ref, log_ref, out_ref, a_ref, b_ref, l_ref, *t_refs):
    parts = part_ref[...]
    top = jnp.max(parts, 0)
    total = top + jnp.log2(jnp.sum(jnp.exp2(parts - top[None]), 0))
    total = jnp.concatenate([total[k : k + 1, :] for k in range(total.shape[0])], 1) + log_n
    total_ref[...] = total
    x, y = x_ref[...], y_ref[...]
    pot_ref[...] = jnp.sum(x * x, 0, keepdims=True) - LN * total
    bound = (jnp.sum(y * y, 0, keepdims=True) - g_ref[...]) * C2 - log_n
    a_ref[...] = first_side(x * (2 * C2), -total).T
    b_ref[...] = second_side(y, -bound)
    log_sums(a_ref, b_ref, t_refs, l_ref)
    logs = l_ref[...] + bound
    log_ref[...] = logs
    for k in range(out_ref.shape[1]):
        out_ref[0, k : k + 1, :] = cut(logs, k)
    for d in range(1, out_ref.shape[0]):
        out_ref[d] = out_ref[0]


def column_images(core_ref, x_ref, y_ref, total_ref, log_ref, keep_ref, send_ref, a_ref, b_ref, v_ref, o_ref, *t_refs):
    x = x_ref[...]
    a_ref[...] = first_side(x * (2 * C2), -total_ref[...]).T
    b_ref[...] = second_side(y_ref[...], -log_ref[...])
    v_ref[...] = coordinates(x)
    weighted(a_ref, b_ref, v_ref, t_refs, o_ref)
    half = o_ref.shape[1] // 2
    for out_ref, side in ((send_ref, 1 - core_ref[0]), (keep_ref, core_ref[0])):
        for q in range(out_ref.shape[0]):
            cols = pl.ds(pl.multiple_of(side * half + q * LANES, LANES), LANES)
            out_ref[q, 0:K, :] = (o_ref[0:K, cols] + o_ref[K : 2 * K, cols]) / o_ref[2 * K : 2 * K + 1, cols]
            out_ref[q, K : K + 8, :] = jnp.broadcast_to(log_ref[:, cols], (8, LANES))


def merge(logs, images):
    top = functools.reduce(jnp.maximum, logs)
    shares = [jnp.exp2(one - top) for one in logs]
    mass = functools.reduce(jnp.add, shares)
    image = functools.reduce(jnp.add, [w * i for w, i in zip(shares, images)])
    return top + jnp.log2(mass), image / mass


def merge_pair(one_ref, two_ref, out_ref):
    logs = [ref[:, K : K + 8, :][:, 0:1, :] for ref in (one_ref, two_ref)]
    log, image = merge(logs, [one_ref[:, 0:K, :], two_ref[:, 0:K, :]])
    out_ref[:, 0:K, :] = image
    out_ref[:, K : K + 8, :] = jnp.broadcast_to(log, (out_ref.shape[0], 8, LANES))


def merge_chunk(part_ref, out_ref):
    n = part_ref.shape[0]
    _, image = merge([part_ref[d, K : K + 1, :] for d in range(n)], [part_ref[d, 0:K, :] for d in range(n)])
    for d in range(n):
        out_ref[d] = image


def merge_logs(part_ref, out_ref):
    n = part_ref.shape[0]
    top = functools.reduce(jnp.maximum, [part_ref[d] for d in range(n)])
    out_ref[...] = top + jnp.log2(functools.reduce(jnp.add, [jnp.exp2(part_ref[d] - top) for d in range(n)]))


def row_images(log_n, side_ref, x_ref, y_ref, total_ref, mine_ref, other_ref, pot_ref, out_ref, a_ref, b_ref, v_ref, o_ref, *t_refs):
    mine, other = mine_ref[...], other_ref[...]
    top = jnp.maximum(mine, other)
    logs = top + jnp.log2(jnp.exp2(mine - top) + jnp.exp2(other - top))
    logs = jnp.concatenate([logs[k : k + 1, :] for k in range(logs.shape[0])], 1)
    y = y_ref[...]
    pot_ref[...] = jnp.sum(y * y, 0, keepdims=True) - LN * (logs + log_n)
    half = o_ref.shape[1]
    cols = pl.ds(pl.multiple_of(side_ref[0] * half, half), half)
    a_ref[...] = first_side(y, -logs).T
    b_ref[...] = second_side(x_ref[:, cols] * (2 * C2), LIFT - total_ref[:, cols])
    v_ref[...] = coordinates(y)
    weighted(a_ref, b_ref, v_ref, t_refs, o_ref)
    tiles = half // LANES
    for k in range(tiles):
        lanes = slice(k * LANES, (k + 1) * LANES)
        for r in range(0, K, 8):
            out_ref[r * tiles + 8 * k : r * tiles + 8 * k + 8, :] = o_ref[r : r + 8, lanes] + o_ref[K + r : K + r + 8, lanes]
        out_ref[K * tiles + k : K * tiles + k + 1, :] = o_ref[2 * K : 2 * K + 1, lanes]
    out_ref[K * tiles + tiles :, :] = jnp.ones((out_ref.shape[0] - (K + 1) * tiles, LANES), F32)


def add_divide(one_ref, two_ref, out_ref):
    rows = out_ref.shape[0]
    tiles = rows // K
    mass = one_ref[rows : rows + 8, :] + two_ref[rows : rows + 8, :]
    for k in range(tiles):
        under = jnp.broadcast_to(mass[k : k + 1, :], (8, LANES))
        for r in range(0, K, 8):
            at = slice(r * tiles + 8 * k, r * tiles + 8 * k + 8)
            out_ref[at, :] = (one_ref[at, :] + two_ref[at, :]) / under


def lay_rows(side_ref, mine_ref, other_ref, out_ref):
    half = out_ref.shape[1] // 2
    tiles = half // LANES
    for side, ref in ((side_ref[0], mine_ref), (1 - side_ref[0], other_ref)):
        for k in range(tiles):
            cols = pl.ds(pl.multiple_of(side * half + k * LANES, LANES), LANES)
            for r in range(0, K, 8):
                out_ref[r : r + 8, cols] = ref[r * tiles + 8 * k : r * tiles + 8 * k + 8, :]


def lay_columns(core_ref, mine_ref, other_ref, out_ref):
    half = out_ref.shape[1] // 2
    for side, ref in ((core_ref[0], mine_ref), (1 - core_ref[0], other_ref)):
        for q in range(ref.shape[0]):
            out_ref[:, pl.ds(pl.multiple_of(side * half + q * LANES, LANES), LANES)] = ref[q]


def call(kernel, ins, outs, scratch=()):
    return pl.pallas_call(
        kernel,
        out_shape=tuple(jax.ShapeDtypeStruct(shape, F32) for shape in outs),
        in_specs=[SM if spec == "s" else VM for spec in ins],
        out_specs=tuple(VM for _ in outs),
        scratch_shapes=[pltpu.VMEM(shape, dtype) for shape, dtype in scratch],
        compiler_params=pltpu.CompilerParams(vmem_limit_bytes=50 << 20),
    )


def solution(mesh):
    n_src, n_tgt = mesh.shape["src"], mesh.shape["tgt"]
    pairs, ring = n_src // 2, n_tgt // 2
    across = [[c + 2 * q for q in range(pairs)] for c in range(2)]
    swap = [(i, i ^ 1) for i in range(n_src)]
    over = [(i, (i + ring) % n_tgt) for i in range(n_tgt)]
    near = [(i, i ^ 1) for i in range(n_tgt)]
    far = [(i, i ^ 3) for i in range(n_tgt)]

    def shards(x, y, g):
        ns, nt = x.shape[1], y.shape[1]
        rows, cols = ns // LANES, nt // LANES
        core = (lax.axis_index("src") & 1).astype(jnp.int32).reshape(1)
        side = (lax.axis_index("tgt") // ring).astype(jnp.int32).reshape(1)
        g = g.reshape(1, nt)
        by_source = [((ns, KD), BF), ((KD, nt), BF)]
        chunk = (pairs, K + 8, LANES)

        (part,) = call(
            row_logs, "vvv", [(n_tgt, rows, LANES)], [((nt, KD), BF), ((KD, ns), BF), ((1, ns), F32), BLOCK, BLOCK]
        )(x, y, g)
        part = lax.all_to_all(part, "tgt", 0, 0, tiled=True)

        source_potential, total, logs, part = call(
            functools.partial(column_logs, math.log2(ns * n_src)),
            "vvvv",
            [(1, ns), (1, ns), (1, nt), (pairs, cols, LANES)],
            by_source + [((1, nt), F32), BLOCK, BLOCK],
        )(x, y, g, part)
        part = lax.all_to_all(part, "src", 0, 0, axis_index_groups=across, tiled=True)
        (mine,) = call(merge_logs, "v", [(cols, LANES)])(part)
        other = lax.ppermute(mine, "src", swap)

        keep, send = call(
            column_images, "svvvv", [chunk, chunk], by_source + [((80, ns), BF), ((80, nt), F32), BLOCK, BLOCK]
        )(core, x, y, total, logs)
        (image,) = call(merge_pair, "vv", [chunk])(keep, lax.ppermute(send, "src", swap))
        image = lax.all_to_all(image, "src", 0, 0, axis_index_groups=across, tiled=True)

        half = ns // 2
        tall = (K * half) // LANES
        images = call(
            functools.partial(row_images, math.log2(nt * n_tgt)),
            "svvvvv",
            [(1, nt), (tall + 8, LANES)],
            [((nt, KD), BF), ((KD, half), BF), ((80, nt), BF), ((80, half), F32), BLOCK, BLOCK],
        )
        target_potential, sent = images(1 - side, x, y, total, mine, other)
        sent = lax.ppermute(sent, "tgt", over)
        _, held = images(side, x, y, total, mine, other)
        held = held + sent
        held = held + lax.ppermute(held, "tgt", near)
        (held,) = call(add_divide, "vv", [(tall, LANES)])(held, lax.ppermute(held, "tgt", far))
        (source_image,) = call(lay_rows, "svv", [(K, ns)])(side, held, lax.ppermute(held, "tgt", over))

        (image,) = call(merge_chunk, "v", [(pairs, K, LANES)])(image)
        image = lax.all_to_all(image, "src", 0, 0, axis_index_groups=across, tiled=True)
        (target_image,) = call(lay_columns, "svv", [(K, nt)])(core, image, lax.ppermute(image, "src", swap))
        return source_potential.reshape(ns), target_potential.reshape(nt), source_image, target_image

    return jax.shard_map(
        shards,
        mesh=mesh,
        in_specs=(P(None, "src"), P(None, "tgt"), P("tgt")),
        out_specs=(P("src"), P("tgt"), P(None, "src"), P(None, "tgt")),
        check_vma=False,
    )
```

```python
import functools
import math

import jax
import jax.numpy as jnp
from jax import lax
from jax.experimental import pallas as pl
from jax.experimental.pallas import tpu as pltpu
from jax.sharding import PartitionSpec as P

EPS = 0.05
C2 = 1.4426950408889634 / EPS
LN = EPS * math.log(2.0)
LEAST = 2.0**-80
LIFT = 64.0
BF = jnp.bfloat16
F32 = jnp.float32
K = 32
KD = 8 * K
VM = pl.BlockSpec(memory_space=pltpu.VMEM)
SM = pl.BlockSpec(memory_space=pltpu.SMEM)
LANES = 128
TALL, WIDE = 1024, 512
BLOCK = ((TALL, WIDE), F32)


def thirds(v):
    hi = v.astype(BF)
    rest = v - hi.astype(F32)
    mid = rest.astype(BF)
    return hi, mid, (rest - mid.astype(F32)).astype(BF)


def halves(v):
    hi = v.astype(BF)
    return hi, (v - hi.astype(F32)).astype(BF)


def offsets(b, first):
    hi, mid, lo = (part.astype(F32) for part in thirds(b))
    row = lax.broadcasted_iota(jnp.int32, (2 * K, b.shape[1]), 0)
    row, one = (row, row - 3) if first else (row - 3, row)
    value = jnp.where(row == 0, hi, jnp.where(row == 1, mid, jnp.where(row == 2, lo, 0.0)))
    return jnp.where((one >= 0) & (one < 3), 1.0, value).astype(BF)


def first_side(v, b):
    hi, mid, lo = thirds(v)
    return jnp.concatenate([hi, hi, hi, mid, mid, lo, offsets(b, True)], 0)


def second_side(v, b):
    hi, mid, lo = thirds(v)
    return jnp.concatenate([hi, mid, lo, hi, mid, hi, offsets(b, False)], 0)


def coordinates(v):
    hi, lo = halves(v)
    return jnp.concatenate([hi, lo, jnp.ones((K // 2, v.shape[1]), BF)], 0)


def cut(tiles, k):
    return tiles[:, k * LANES : (k + 1) * LANES]


def blocks(a_ref, b_ref, t_refs, first, use):
    tall, wide = t_refs[0].shape
    places = [(r, c) for c in range(first, first + b_ref.shape[1], wide) for r in range(0, a_ref.shape[0], tall)]

    def fill(i):
        r, c = places[i]
        t_refs[i % 2][...] = jnp.dot(a_ref[r : r + tall, :], b_ref[:, c : c + wide], preferred_element_type=F32)

    fill(0)
    for i, (r, c) in enumerate(places):
        if i + 1 < len(places):
            fill(i + 1)
        use(t_refs[i % 2], slice(r, r + tall), slice(c, c + wide))


def log_sums(a_ref, b_ref, t_refs, l_ref):
    tall, wide = t_refs[0].shape

    def use(t_ref, rows, cols):
        part = jnp.sum(jnp.exp2(t_ref[...]), 0, keepdims=True)
        l_ref[:, cols] = part if rows.start == 0 else l_ref[:, cols] + part

    blocks(a_ref, b_ref, t_refs, 0, use)
    least = jnp.min(l_ref[...])
    l_ref[...] = jnp.log2(l_ref[...])

    @pl.when(least < LEAST)
    def _():
        t_ref = t_refs[0]

        def column(c, _):
            cols = pl.ds(pl.multiple_of(c * wide, wide), wide)

            def fill(r):
                rows = pl.ds(pl.multiple_of(r * tall, tall), tall)
                t_ref[...] = jnp.dot(a_ref[rows, :], b_ref[:, cols], preferred_element_type=F32)

            def highest(r, peak):
                fill(r)
                return jnp.maximum(peak, jnp.max(t_ref[...], 0, keepdims=True))

            count = a_ref.shape[0] // tall
            peak = lax.fori_loop(0, count, highest, jnp.full((1, wide), -1e30, F32))

            def add(r, total):
                fill(r)
                return total + jnp.sum(jnp.exp2(t_ref[...] - peak), 0, keepdims=True)

            l_ref[:, cols] = peak + jnp.log2(lax.fori_loop(0, count, add, jnp.zeros((1, wide), F32)))
            return 0

        lax.fori_loop(0, b_ref.shape[1] // wide, column, 0)


def weighted(a_ref, b_ref, v_ref, t_refs, o_ref):
    def use(t_ref, rows, cols):
        hi, lo = halves(jnp.exp2(t_ref[...]))
        part = jnp.dot(v_ref[:, rows], hi, preferred_element_type=F32)
        part += jnp.dot(v_ref[:, rows], lo, preferred_element_type=F32)
        o_ref[:, cols] = part if rows.start == 0 else o_ref[:, cols] + part

    blocks(a_ref, b_ref, t_refs, 0, use)


def row_logs(x_hbm, y_hbm, g_hbm, out_ref, x_ref, y_ref, g_ref, a_ref, b_ref, l_ref, t0_ref, t1_ref, sems):
    t_refs = (t0_ref, t1_ref)
    sides = ((y_hbm, y_ref), (x_hbm, x_ref), (g_hbm, g_ref))
    copies = [pltpu.make_async_copy(*pair, sems.at[i]) for i, pair in enumerate(sides)]
    for copy in copies:
        copy.start()
    for copy in copies:
        copy.wait()
    x, y = x_ref[...], y_ref[...]
    y_sq = jnp.sum(y * y, 0, keepdims=True)
    lift = (g_ref[...] - y_sq) * C2
    longest = jnp.sqrt(jnp.sum(x * x, 0, keepdims=True)) * jnp.sqrt(jnp.max(y_sq, 1, keepdims=True))
    bound = jnp.max(lift, 1, keepdims=True) + 2 * C2 * longest
    a_ref[...] = first_side(y, lift).T
    b_ref[...] = second_side(x * (2 * C2), -bound)
    log_sums(a_ref, b_ref, t_refs, l_ref)
    total = l_ref[...] + bound
    for k in range(out_ref.shape[1]):
        for d in range(out_ref.shape[0]):
            out_ref[d, k : k + 1, :] = cut(total, k)


def column_logs(log_n, x_ref, y_ref, g_ref, part_ref, pot_ref, total_ref, log_ref, out_ref, a_ref, b_ref, l_ref, *t_refs):
    parts = part_ref[...]
    top = jnp.max(parts, 0)
    total = top + jnp.log2(jnp.sum(jnp.exp2(parts - top[None]), 0))
    total = jnp.concatenate([total[k : k + 1, :] for k in range(total.shape[0])], 1) + log_n
    total_ref[...] = total
    x, y = x_ref[...], y_ref[...]
    pot_ref[...] = jnp.sum(x * x, 0, keepdims=True) - LN * total
    bound = (jnp.sum(y * y, 0, keepdims=True) - g_ref[...]) * C2 - log_n
    a_ref[...] = first_side(x * (2 * C2), -total).T
    b_ref[...] = second_side(y, -bound)
    log_sums(a_ref, b_ref, t_refs, l_ref)
    logs = l_ref[...] + bound
    log_ref[...] = logs
    for k in range(out_ref.shape[1]):
        out_ref[0, k : k + 1, :] = cut(logs, k)
    for d in range(1, out_ref.shape[0]):
        out_ref[d] = out_ref[0]


def column_images(core_ref, x_ref, y_ref, total_ref, log_ref, keep_ref, send_ref, a_ref, b_ref, v_ref, o_ref, *t_refs):
    x = x_ref[...]
    a_ref[...] = first_side(x * (2 * C2), -total_ref[...]).T
    b_ref[...] = second_side(y_ref[...], -log_ref[...])
    v_ref[...] = coordinates(x)
    weighted(a_ref, b_ref, v_ref, t_refs, o_ref)
    half = o_ref.shape[1] // 2
    for out_ref, side in ((send_ref, 1 - core_ref[0]), (keep_ref, core_ref[0])):
        for q in range(out_ref.shape[0]):
            cols = pl.ds(pl.multiple_of(side * half + q * LANES, LANES), LANES)
            out_ref[q, 0:K, :] = (o_ref[0:K, cols] + o_ref[K : 2 * K, cols]) / o_ref[2 * K : 2 * K + 1, cols]
            out_ref[q, K : K + 8, :] = jnp.broadcast_to(log_ref[:, cols], (8, LANES))


def merge(logs, images):
    top = functools.reduce(jnp.maximum, logs)
    shares = [jnp.exp2(one - top) for one in logs]
    mass = functools.reduce(jnp.add, shares)
    image = functools.reduce(jnp.add, [w * i for w, i in zip(shares, images)])
    return top + jnp.log2(mass), image / mass


def merge_pair(one_ref, two_ref, after_ref, out_ref):
    pair = (one_ref, two_ref)
    log, image = merge([ref[:, K : K + 8, :][:, 0:1, :] for ref in pair], [ref[:, 0:K, :] for ref in pair])
    out_ref[:, 0:K, :] = image
    out_ref[:, K : K + 8, :] = jnp.broadcast_to(log, (out_ref.shape[0], 8, LANES))


def merge_chunk(part_ref, after_ref, out_ref):
    n = part_ref.shape[0]
    _, image = merge([part_ref[d, K : K + 1, :] for d in range(n)], [part_ref[d, 0:K, :] for d in range(n)])
    for d in range(out_ref.shape[0]):
        out_ref[d] = image


def merge_logs(part_ref, out_ref):
    n = part_ref.shape[0]
    top = functools.reduce(jnp.maximum, [part_ref[d] for d in range(n)])
    out_ref[...] = top + jnp.log2(functools.reduce(jnp.add, [jnp.exp2(part_ref[d] - top) for d in range(n)]))


def row_images(log_n, side_ref, x_ref, y_ref, total_ref, mine_ref, other_ref, after_ref, pot_ref, out_ref, a_ref, b_ref, v_ref, o_ref, *t_refs):
    mine, other = mine_ref[...], other_ref[...]
    top = jnp.maximum(mine, other)
    logs = top + jnp.log2(jnp.exp2(mine - top) + jnp.exp2(other - top))
    logs = jnp.concatenate([logs[k : k + 1, :] for k in range(logs.shape[0])], 1)
    y = y_ref[...]
    pot_ref[...] = jnp.sum(y * y, 0, keepdims=True) - LN * (logs + log_n)
    half = o_ref.shape[1]
    cols = pl.ds(pl.multiple_of(side_ref[0] * half, half), half)
    a_ref[...] = first_side(y, -logs).T
    b_ref[...] = second_side(x_ref[:, cols] * (2 * C2), LIFT - total_ref[:, cols])
    v_ref[...] = coordinates(y)
    weighted(a_ref, b_ref, v_ref, t_refs, o_ref)
    tiles = half // LANES
    for k in range(tiles):
        lanes = slice(k * LANES, (k + 1) * LANES)
        for r in range(0, K, 8):
            out_ref[r * tiles + 8 * k : r * tiles + 8 * k + 8, :] = o_ref[r : r + 8, lanes] + o_ref[K + r : K + r + 8, lanes]
        out_ref[K * tiles + k : K * tiles + k + 1, :] = o_ref[2 * K : 2 * K + 1, lanes]
    out_ref[K * tiles + tiles :, :] = jnp.ones((out_ref.shape[0] - (K + 1) * tiles, LANES), F32)


def add_divide(one_ref, two_ref, out_ref):
    rows = out_ref.shape[0]
    tiles = rows // K
    mass = one_ref[rows : rows + 8, :] + two_ref[rows : rows + 8, :]
    for k in range(tiles):
        under = jnp.broadcast_to(mass[k : k + 1, :], (8, LANES))
        for r in range(0, K, 8):
            at = slice(r * tiles + 8 * k, r * tiles + 8 * k + 8)
            out_ref[at, :] = (one_ref[at, :] + two_ref[at, :]) / under


def lay_rows(side_ref, mine_ref, other_ref, out_ref):
    half = out_ref.shape[1] // 2
    tiles = half // LANES
    for side, ref in ((side_ref[0], mine_ref), (1 - side_ref[0], other_ref)):
        for k in range(tiles):
            cols = pl.ds(pl.multiple_of(side * half + k * LANES, LANES), LANES)
            for r in range(0, K, 8):
                out_ref[r : r + 8, cols] = ref[r * tiles + 8 * k : r * tiles + 8 * k + 8, :]


def hold(image_ref, after_ref, out_ref):
    pass


def lay_columns(core_ref, mine_ref, other_ref, out_ref):
    half = out_ref.shape[1] // 2
    for side, ref in ((core_ref[0], mine_ref), (1 - core_ref[0], other_ref)):
        for q in range(ref.shape[0]):
            out_ref[:, pl.ds(pl.multiple_of(side * half + q * LANES, LANES), LANES)] = ref[q]


def call(kernel, ins, outs, scratch=(), copies=0, aliases={}, cost=None):
    return pl.pallas_call(
        kernel,
        out_shape=tuple(jax.ShapeDtypeStruct(shape, F32) for shape in outs),
        in_specs=[{"s": SM, "h": pl.BlockSpec(memory_space=pltpu.HBM), "v": VM}[spec] for spec in ins],
        out_specs=tuple(VM for _ in outs),
        scratch_shapes=[pltpu.VMEM(*one) for one in scratch] + [pltpu.SemaphoreType.DMA((copies,))] * (copies > 0),
        input_output_aliases=aliases,
        cost_estimate=cost,
        compiler_params=pltpu.CompilerParams(vmem_limit_bytes=50 << 20),
    )


def work(pairs, sums):
    return pl.CostEstimate(flops=2 * pairs * (KD + 256 * sums), transcendentals=pairs, bytes_accessed=8 * pairs)


def solution(mesh):
    n_src, n_tgt = mesh.shape["src"], mesh.shape["tgt"]
    pairs, ring = n_src // 2, n_tgt // 2
    across = [[c + 2 * q for q in range(pairs)] for c in range(2)]
    swap = [(i, i ^ 1) for i in range(n_src)]
    over = [(i, (i + ring) % n_tgt) for i in range(n_tgt)]
    near = [(i, i ^ 1) for i in range(n_tgt)]
    far = [(i, i ^ 3) for i in range(n_tgt)]

    def shards(x, y, g):
        ns, nt = x.shape[1], y.shape[1]
        rows, cols = ns // LANES, nt // LANES
        core = (lax.axis_index("src") & 1).astype(jnp.int32).reshape(1)
        side = (lax.axis_index("tgt") // ring).astype(jnp.int32).reshape(1)
        g = g.reshape(1, nt)
        by_source = [((ns, KD), BF), ((KD, nt), BF)]
        chunk = (pairs, K + 8, LANES)

        part, x, y, g = call(
            row_logs,
            "hhh",
            [(n_tgt, rows, LANES), x.shape, y.shape, g.shape],
            [((nt, KD), BF), ((KD, ns), BF), ((1, ns), F32), BLOCK, BLOCK],
            3,
            cost=work(ns * nt, 0),
        )(*(pltpu.with_memory_space_constraint(one, pltpu.HBM) for one in (x, y, g)))
        part = lax.all_to_all(part, "tgt", 0, 0, tiled=True)

        source_potential, total, logs, part = call(
            functools.partial(column_logs, math.log2(ns * n_src)),
            "vvvv",
            [(1, ns), (1, ns), (1, nt), (pairs, cols, LANES)],
            by_source + [((1, nt), F32), BLOCK, BLOCK],
            cost=work(ns * nt, 0),
        )(x, y, g, part)
        part = lax.all_to_all(part, "src", 0, 0, axis_index_groups=across, tiled=True)
        (mine,) = call(merge_logs, "v", [(cols, LANES)])(part)
        other = lax.ppermute(mine, "src", swap)

        keep, send = call(
            column_images,
            "svvvv",
            [chunk, chunk],
            by_source + [((80, ns), BF), ((80, nt), F32), BLOCK, BLOCK],
            cost=work(ns * nt, 2),
        )(core, x, y, total, logs)
        (image,) = call(merge_pair, "vvv", [chunk])(keep, lax.ppermute(send, "src", swap), mine)
        image = lax.all_to_all(image, "src", 0, 0, axis_index_groups=across, tiled=True)

        half = ns // 2
        tall = (K * half) // LANES
        images = call(
            functools.partial(row_images, math.log2(nt * n_tgt)),
            "svvvvvv",
            [(1, nt), (tall + 8, LANES)],
            [((nt, KD), BF), ((KD, half), BF), ((80, nt), BF), ((80, half), F32), BLOCK, BLOCK],
            cost=work(half * nt, 2),
        )
        target_potential, sent = images(1 - side, x, y, total, mine, other, mine)
        _, held = images(side, x, y, total, mine, other, sent)
        sent = lax.ppermute(sent, "tgt", over)
        held = held + sent
        (image,) = call(merge_chunk, "vv", [(pairs, K, LANES)], cost=work(half * nt, 2))(image, held)
        image = lax.all_to_all(image, "src", 0, 0, axis_index_groups=across, tiled=True)
        held = held + lax.ppermute(held, "tgt", near)
        (held,) = call(add_divide, "vv", [(tall, LANES)])(held, lax.ppermute(held, "tgt", far))
        (source_image,) = call(lay_rows, "svv", [(K, ns)])(side, held, lax.ppermute(held, "tgt", over))
        (image,) = call(hold, "vv", [image.shape], aliases={0: 0})(image, source_image)
        (target_image,) = call(lay_columns, "svv", [(K, nt)])(core, image, lax.ppermute(image, "src", swap))
        return source_potential.reshape(ns), target_potential.reshape(nt), source_image, target_image

    return jax.shard_map(
        shards,
        mesh=mesh,
        in_specs=(P(None, "src"), P(None, "tgt"), P("tgt")),
        out_specs=(P("src"), P("tgt"), P(None, "src"), P(None, "tgt")),
        check_vma=False,
    )
```

```python
import functools
import math

import jax
import jax.numpy as jnp
from jax import lax
from jax.experimental import pallas as pl
from jax.experimental.pallas import tpu as pltpu
from jax.sharding import PartitionSpec as P

EPS = 0.05
C2 = 1.4426950408889634 / EPS
LN = EPS * math.log(2.0)
LEAST = 2.0**-80
LIFT = 64.0
BF = jnp.bfloat16
F32 = jnp.float32
K = 32
KD = 8 * K
VM = pl.BlockSpec(memory_space=pltpu.VMEM)
SM = pl.BlockSpec(memory_space=pltpu.SMEM)
LANES = 128
TALL, WIDE = 1024, 512
BLOCK = ((TALL, WIDE), F32)


def thirds(v):
    hi = v.astype(BF)
    rest = v - hi.astype(F32)
    mid = rest.astype(BF)
    return hi, mid, (rest - mid.astype(F32)).astype(BF)


def halves(v):
    hi = v.astype(BF)
    return hi, (v - hi.astype(F32)).astype(BF)


def offsets(b, first):
    hi, mid, lo = (part.astype(F32) for part in thirds(b))
    row = lax.broadcasted_iota(jnp.int32, (2 * K, b.shape[1]), 0)
    row, one = (row, row - 3) if first else (row - 3, row)
    value = jnp.where(row == 0, hi, jnp.where(row == 1, mid, jnp.where(row == 2, lo, 0.0)))
    return jnp.where((one >= 0) & (one < 3), 1.0, value).astype(BF)


def first_side(v, b):
    hi, mid, lo = thirds(v)
    return jnp.concatenate([hi, hi, hi, mid, mid, lo, offsets(b, True)], 0)


def second_side(v, b):
    hi, mid, lo = thirds(v)
    return jnp.concatenate([hi, mid, lo, hi, mid, hi, offsets(b, False)], 0)


def coordinates(v):
    hi, lo = halves(v)
    return jnp.concatenate([hi, lo, jnp.ones((K // 2, v.shape[1]), BF)], 0)


def cut(tiles, k):
    return tiles[:, k * LANES : (k + 1) * LANES]


def blocks(a_ref, b_ref, t_refs, first, use):
    tall, wide = t_refs[0].shape
    places = [(r, c) for c in range(first, first + b_ref.shape[1], wide) for r in range(0, a_ref.shape[0], tall)]

    def fill(i):
        r, c = places[i]
        t_refs[i % 2][...] = jnp.dot(a_ref[r : r + tall, :], b_ref[:, c : c + wide], preferred_element_type=F32)

    fill(0)
    for i, (r, c) in enumerate(places):
        if i + 1 < len(places):
            fill(i + 1)
        use(t_refs[i % 2], slice(r, r + tall), slice(c, c + wide))


def log_sums(a_ref, b_ref, t_refs, l_ref):
    tall, wide = t_refs[0].shape

    def use(t_ref, rows, cols):
        part = jnp.sum(jnp.exp2(t_ref[...]), 0, keepdims=True)
        l_ref[:, cols] = part if rows.start == 0 else l_ref[:, cols] + part

    blocks(a_ref, b_ref, t_refs, 0, use)
    least = jnp.min(l_ref[...])
    l_ref[...] = jnp.log2(l_ref[...])

    @pl.when(least < LEAST)
    def _():
        t_ref = t_refs[0]

        def column(c, _):
            cols = pl.ds(pl.multiple_of(c * wide, wide), wide)

            def fill(r):
                rows = pl.ds(pl.multiple_of(r * tall, tall), tall)
                t_ref[...] = jnp.dot(a_ref[rows, :], b_ref[:, cols], preferred_element_type=F32)

            def highest(r, peak):
                fill(r)
                return jnp.maximum(peak, jnp.max(t_ref[...], 0, keepdims=True))

            count = a_ref.shape[0] // tall
            peak = lax.fori_loop(0, count, highest, jnp.full((1, wide), -1e30, F32))

            def add(r, total):
                fill(r)
                return total + jnp.sum(jnp.exp2(t_ref[...] - peak), 0, keepdims=True)

            l_ref[:, cols] = peak + jnp.log2(lax.fori_loop(0, count, add, jnp.zeros((1, wide), F32)))
            return 0

        lax.fori_loop(0, b_ref.shape[1] // wide, column, 0)


def weighted(a_ref, b_ref, v_ref, t_refs, o_ref):
    def use(t_ref, rows, cols):
        hi, lo = halves(jnp.exp2(t_ref[...]))
        part = jnp.dot(v_ref[:, rows], hi, preferred_element_type=F32)
        part += jnp.dot(v_ref[:, rows], lo, preferred_element_type=F32)
        o_ref[:, cols] = part if rows.start == 0 else o_ref[:, cols] + part

    blocks(a_ref, b_ref, t_refs, 0, use)


def row_logs(x_hbm, y_hbm, g_hbm, out_ref, x_ref, y_ref, g_ref, a_ref, b_ref, l_ref, t0_ref, t1_ref, sems):
    t_refs = (t0_ref, t1_ref)
    sides = ((y_hbm, y_ref), (x_hbm, x_ref), (g_hbm, g_ref))
    copies = [pltpu.make_async_copy(*pair, sems.at[i]) for i, pair in enumerate(sides)]
    for copy in copies:
        copy.start()
    for copy in copies:
        copy.wait()
    x, y = x_ref[...], y_ref[...]
    y_sq = jnp.sum(y * y, 0, keepdims=True)
    lift = (g_ref[...] - y_sq) * C2
    longest = jnp.sqrt(jnp.sum(x * x, 0, keepdims=True)) * jnp.sqrt(jnp.max(y_sq, 1, keepdims=True))
    bound = jnp.max(lift, 1, keepdims=True) + 2 * C2 * longest
    a_ref[...] = first_side(y, lift).T
    b_ref[...] = second_side(x * (2 * C2), -bound)
    log_sums(a_ref, b_ref, t_refs, l_ref)
    total = l_ref[...] + bound
    for k in range(out_ref.shape[1]):
        for d in range(out_ref.shape[0]):
            out_ref[d, k : k + 1, :] = cut(total, k)


def column_logs(log_n, x_ref, y_ref, g_ref, part_ref, pot_ref, total_ref, log_ref, out_ref, a_ref, b_ref, l_ref, *t_refs):
    parts = part_ref[...]
    top = jnp.max(parts, 0)
    total = top + jnp.log2(jnp.sum(jnp.exp2(parts - top[None]), 0))
    total = jnp.concatenate([total[k : k + 1, :] for k in range(total.shape[0])], 1) + log_n
    total_ref[...] = total
    x, y = x_ref[...], y_ref[...]
    pot_ref[...] = jnp.sum(x * x, 0, keepdims=True) - LN * total
    bound = (jnp.sum(y * y, 0, keepdims=True) - g_ref[...]) * C2 - log_n
    a_ref[...] = first_side(x * (2 * C2), -total).T
    b_ref[...] = second_side(y, -bound)
    log_sums(a_ref, b_ref, t_refs, l_ref)
    logs = l_ref[...] + bound
    log_ref[...] = logs
    for k in range(out_ref.shape[1]):
        out_ref[0, k : k + 1, :] = cut(logs, k)
    for d in range(1, out_ref.shape[0]):
        out_ref[d] = out_ref[0]


def column_images(core_ref, x_ref, y_ref, total_ref, log_ref, keep_ref, send_ref, a_ref, b_ref, v_ref, o_ref, *t_refs):
    x = x_ref[...]
    a_ref[...] = first_side(x * (2 * C2), -total_ref[...]).T
    b_ref[...] = second_side(y_ref[...], -log_ref[...])
    v_ref[...] = coordinates(x)
    weighted(a_ref, b_ref, v_ref, t_refs, o_ref)
    half = o_ref.shape[1] // 2
    for out_ref, side in ((send_ref, 1 - core_ref[0]), (keep_ref, core_ref[0])):
        for q in range(out_ref.shape[0]):
            cols = pl.ds(pl.multiple_of(side * half + q * LANES, LANES), LANES)
            out_ref[q, 0:K, :] = (o_ref[0:K, cols] + o_ref[K : 2 * K, cols]) / o_ref[2 * K : 2 * K + 1, cols]
            out_ref[q, K : K + 8, :] = jnp.broadcast_to(log_ref[:, cols], (8, LANES))


def merge(logs, images):
    top = functools.reduce(jnp.maximum, logs)
    shares = [jnp.exp2(one - top) for one in logs]
    mass = functools.reduce(jnp.add, shares)
    image = functools.reduce(jnp.add, [w * i for w, i in zip(shares, images)])
    return top + jnp.log2(mass), image / mass


def merge_pair(one_ref, two_ref, after_ref, out_ref):
    pair = (one_ref, two_ref)
    log, image = merge([ref[:, K : K + 8, :][:, 0:1, :] for ref in pair], [ref[:, 0:K, :] for ref in pair])
    out_ref[:, 0:K, :] = image
    out_ref[:, K : K + 8, :] = jnp.broadcast_to(log, (out_ref.shape[0], 8, LANES))


def merge_chunk(part_ref, after_ref, out_ref):
    n = part_ref.shape[0]
    _, image = merge([part_ref[d, K : K + 1, :] for d in range(n)], [part_ref[d, 0:K, :] for d in range(n)])
    for d in range(out_ref.shape[0]):
        out_ref[d] = image


def merge_logs(part_ref, out_ref):
    n = part_ref.shape[0]
    top = functools.reduce(jnp.maximum, [part_ref[d] for d in range(n)])
    out_ref[...] = top + jnp.log2(functools.reduce(jnp.add, [jnp.exp2(part_ref[d] - top) for d in range(n)]))


def row_images(log_n, side_ref, x_ref, y_ref, total_ref, mine_ref, other_ref, after_ref, pot_ref, out_ref, a_ref, b_ref, v_ref, o_ref, *t_refs):
    mine, other = mine_ref[...], other_ref[...]
    top = jnp.maximum(mine, other)
    logs = top + jnp.log2(jnp.exp2(mine - top) + jnp.exp2(other - top))
    logs = jnp.concatenate([logs[k : k + 1, :] for k in range(logs.shape[0])], 1)
    y = y_ref[...]
    pot_ref[...] = jnp.sum(y * y, 0, keepdims=True) - LN * (logs + log_n)
    half = o_ref.shape[1]
    cols = pl.ds(pl.multiple_of(side_ref[0] * half, half), half)
    a_ref[...] = first_side(y, -logs).T
    b_ref[...] = second_side(x_ref[:, cols] * (2 * C2), LIFT - total_ref[:, cols])
    v_ref[...] = coordinates(y)
    weighted(a_ref, b_ref, v_ref, t_refs, o_ref)
    tiles = half // LANES
    for k in range(tiles):
        lanes = slice(k * LANES, (k + 1) * LANES)
        for r in range(0, K, 8):
            out_ref[r * tiles + 8 * k : r * tiles + 8 * k + 8, :] = o_ref[r : r + 8, lanes] + o_ref[K + r : K + r + 8, lanes]
        out_ref[K * tiles + k : K * tiles + k + 1, :] = o_ref[2 * K : 2 * K + 1, lanes]
    out_ref[K * tiles + tiles :, :] = jnp.ones((out_ref.shape[0] - (K + 1) * tiles, LANES), F32)


def add_divide(one_ref, two_ref, out_ref):
    rows = out_ref.shape[0]
    tiles = rows // K
    mass = one_ref[rows : rows + 8, :] + two_ref[rows : rows + 8, :]
    for k in range(tiles):
        under = jnp.broadcast_to(mass[k : k + 1, :], (8, LANES))
        for r in range(0, K, 8):
            at = slice(r * tiles + 8 * k, r * tiles + 8 * k + 8)
            out_ref[at, :] = (one_ref[at, :] + two_ref[at, :]) / under


def lay_rows(side_ref, mine_ref, other_ref, out_ref):
    half = out_ref.shape[1] // 2
    tiles = half // LANES
    for side, ref in ((side_ref[0], mine_ref), (1 - side_ref[0], other_ref)):
        for k in range(tiles):
            cols = pl.ds(pl.multiple_of(side * half + k * LANES, LANES), LANES)
            for r in range(0, K, 8):
                out_ref[r : r + 8, cols] = ref[r * tiles + 8 * k : r * tiles + 8 * k + 8, :]


def hold(image_ref, after_ref, out_ref):
    pass


def lay_columns(core_ref, mine_ref, other_ref, out_ref):
    half = out_ref.shape[1] // 2
    for side, ref in ((core_ref[0], mine_ref), (1 - core_ref[0], other_ref)):
        for q in range(ref.shape[0]):
            out_ref[:, pl.ds(pl.multiple_of(side * half + q * LANES, LANES), LANES)] = ref[q]


def call(kernel, ins, outs, scratch=(), copies=0, aliases={}, cost=None):
    return pl.pallas_call(
        kernel,
        out_shape=tuple(jax.ShapeDtypeStruct(shape, F32) for shape in outs),
        in_specs=[{"s": SM, "h": pl.BlockSpec(memory_space=pltpu.HBM), "v": VM}[spec] for spec in ins],
        out_specs=tuple(VM for _ in outs),
        scratch_shapes=[pltpu.VMEM(*one) for one in scratch] + [pltpu.SemaphoreType.DMA((copies,))] * (copies > 0),
        input_output_aliases=aliases,
        cost_estimate=cost,
        compiler_params=pltpu.CompilerParams(vmem_limit_bytes=50 << 20),
    )


def work(pairs, sums):
    return pl.CostEstimate(flops=2 * pairs * (KD + 256 * sums), transcendentals=pairs, bytes_accessed=8 * pairs)


def solution(mesh):
    n_src, n_tgt = mesh.shape["src"], mesh.shape["tgt"]
    pairs, ring = n_src // 2, n_tgt // 2
    across = [[c + 2 * q for q in range(pairs)] for c in range(2)]
    swap = [(i, i ^ 1) for i in range(n_src)]
    over = [(i, (i + ring) % n_tgt) for i in range(n_tgt)]
    near = [(i, i ^ 1) for i in range(n_tgt)]
    far = [(i, i ^ 3) for i in range(n_tgt)]

    def shards(x, y, g):
        ns, nt = x.shape[1], y.shape[1]
        rows, cols = ns // LANES, nt // LANES
        core = (lax.axis_index("src") & 1).astype(jnp.int32).reshape(1)
        side = (lax.axis_index("tgt") // ring).astype(jnp.int32).reshape(1)
        g = g.reshape(1, nt)
        by_source = [((ns, KD), BF), ((KD, nt), BF)]
        chunk = (pairs, K + 8, LANES)

        part, x, y, g = call(
            row_logs,
            "hhh",
            [(n_tgt, rows, LANES), x.shape, y.shape, g.shape],
            [((nt, KD), BF), ((KD, ns), BF), ((1, ns), F32), BLOCK, BLOCK],
            3,
            cost=work(ns * nt, 0),
        )(*(pltpu.with_memory_space_constraint(one, pltpu.HBM) for one in (x, y, g)))
        part = lax.all_to_all(part, "tgt", 0, 0, tiled=True)

        source_potential, total, logs, part = call(
            functools.partial(column_logs, math.log2(ns * n_src)),
            "vvvv",
            [(1, ns), (1, ns), (1, nt), (pairs, cols, LANES)],
            by_source + [((1, nt), F32), BLOCK, BLOCK],
            cost=work(ns * nt, 0),
        )(x, y, g, part)
        part = lax.all_to_all(part, "src", 0, 0, axis_index_groups=across, tiled=True)
        (mine,) = call(merge_logs, "v", [(cols, LANES)])(part)
        other = lax.ppermute(mine, "src", swap)

        keep, send = call(
            column_images,
            "svvvv",
            [chunk, chunk],
            by_source + [((80, ns), BF), ((80, nt), F32), BLOCK, BLOCK],
            cost=work(ns * nt, 2),
        )(core, x, y, total, logs)
        (image,) = call(merge_pair, "vvv", [chunk])(keep, lax.ppermute(send, "src", swap), mine)
        image = lax.all_to_all(image, "src", 0, 0, axis_index_groups=across, tiled=True)

        half = ns // 2
        tall = (K * half) // LANES
        images = call(
            functools.partial(row_images, math.log2(nt * n_tgt)),
            "svvvvvv",
            [(1, nt), (tall + 8, LANES)],
            [((nt, KD), BF), ((KD, half), BF), ((80, nt), BF), ((80, half), F32), BLOCK, BLOCK],
            cost=work(half * nt, 2),
        )
        target_potential, sent = images(1 - side, x, y, total, mine, other, mine)
        _, held = images(side, x, y, total, mine, other, sent)
        sent = lax.ppermute(sent, "tgt", over)
        held = held + sent
        (image,) = call(merge_chunk, "vv", [(pairs, K, LANES)], cost=work(half * nt, 2))(image, held)
        image = lax.all_to_all(image, "src", 0, 0, axis_index_groups=across, tiled=True)
        held = held + lax.ppermute(held, "tgt", near)
        (held,) = call(add_divide, "vv", [(tall, LANES)], cost=work(half * nt, 2))(held, lax.ppermute(held, "tgt", far))
        sent = lax.ppermute(held, "tgt", over)
        (source_image,) = call(lay_rows, "svv", [(K, ns)], cost=work(half * nt, 2))(side, held, sent)
        (image,) = call(hold, "vv", [image.shape], aliases={0: 0})(image, sent)
        (target_image,) = call(lay_columns, "svv", [(K, nt)])(core, image, lax.ppermute(image, "src", swap))
        return source_potential.reshape(ns), target_potential.reshape(nt), source_image, target_image

    return jax.shard_map(
        shards,
        mesh=mesh,
        in_specs=(P(None, "src"), P(None, "tgt"), P("tgt")),
        out_specs=(P("src"), P("tgt"), P(None, "src"), P(None, "tgt")),
        check_vma=False,
    )
```

```python
import functools
import math

import jax
import jax.numpy as jnp
from jax import lax
from jax.experimental import pallas as pl
from jax.experimental.pallas import tpu as pltpu
from jax.sharding import Mesh
from jax.sharding import PartitionSpec as P

EPS = 0.05
C2 = 1.4426950408889634 / EPS
LN = EPS * math.log(2.0)
LEAST = 2.0**-80
LIFT = 64.0
BF = jnp.bfloat16
F32 = jnp.float32
K = 32
KD = 8 * K
VM = pl.BlockSpec(memory_space=pltpu.VMEM)
SM = pl.BlockSpec(memory_space=pltpu.SMEM)
LANES = 128
TALL, WIDE = 1024, 512
BLOCK = ((TALL, WIDE), F32)


def thirds(v):
    hi = v.astype(BF)
    rest = v - hi.astype(F32)
    mid = rest.astype(BF)
    return hi, mid, (rest - mid.astype(F32)).astype(BF)


def halves(v):
    hi = v.astype(BF)
    return hi, (v - hi.astype(F32)).astype(BF)


def offsets(b, first):
    hi, mid, lo = (part.astype(F32) for part in thirds(b))
    row = lax.broadcasted_iota(jnp.int32, (2 * K, b.shape[1]), 0)
    row, one = (row, row - 3) if first else (row - 3, row)
    value = jnp.where(row == 0, hi, jnp.where(row == 1, mid, jnp.where(row == 2, lo, 0.0)))
    return jnp.where((one >= 0) & (one < 3), 1.0, value).astype(BF)


def first_side(v, b):
    hi, mid, lo = thirds(v)
    return jnp.concatenate([hi, hi, hi, mid, mid, lo, offsets(b, True)], 0)


def second_side(v, b):
    hi, mid, lo = thirds(v)
    return jnp.concatenate([hi, mid, lo, hi, mid, hi, offsets(b, False)], 0)


def coordinates(v):
    hi, lo = halves(v)
    return jnp.concatenate([hi, lo, jnp.ones((K // 2, v.shape[1]), BF)], 0)


def cut(tiles, k):
    return tiles[:, k * LANES : (k + 1) * LANES]


def blocks(a_ref, b_ref, t_refs, first, use):
    tall, wide = t_refs[0].shape
    places = [(r, c) for c in range(first, first + b_ref.shape[1], wide) for r in range(0, a_ref.shape[0], tall)]

    def fill(i):
        r, c = places[i]
        t_refs[i % 2][...] = jnp.dot(a_ref[r : r + tall, :], b_ref[:, c : c + wide], preferred_element_type=F32)

    fill(0)
    for i, (r, c) in enumerate(places):
        if i + 1 < len(places):
            fill(i + 1)
        use(t_refs[i % 2], slice(r, r + tall), slice(c, c + wide))


def exact_logs(a_ref, b_ref, t_ref, l_ref):
    tall, wide = t_ref.shape

    def column(c, _):
        cols = pl.ds(pl.multiple_of(c * wide, wide), wide)

        def fill(r):
            rows = pl.ds(pl.multiple_of(r * tall, tall), tall)
            t_ref[...] = jnp.dot(a_ref[rows, :], b_ref[:, cols], preferred_element_type=F32)

        def highest(r, peak):
            fill(r)
            return jnp.maximum(peak, jnp.max(t_ref[...], 0, keepdims=True))

        count = a_ref.shape[0] // tall
        peak = lax.fori_loop(0, count, highest, jnp.full((1, wide), -1e30, F32))

        def add(r, total):
            fill(r)
            return total + jnp.sum(jnp.exp2(t_ref[...] - peak), 0, keepdims=True)

        l_ref[:, cols] = peak + jnp.log2(lax.fori_loop(0, count, add, jnp.zeros((1, wide), F32)))
        return 0

    lax.fori_loop(0, b_ref.shape[1] // wide, column, 0)


def log_sums(a_ref, b_ref, t_refs, l_ref):
    def use(t_ref, rows, cols):
        part = jnp.sum(jnp.exp2(t_ref[...]), 0, keepdims=True)
        l_ref[:, cols] = part if rows.start == 0 else l_ref[:, cols] + part

    blocks(a_ref, b_ref, t_refs, 0, use)
    least = jnp.min(l_ref[...])
    l_ref[...] = jnp.log2(l_ref[...])

    @pl.when(least < LEAST)
    def _():
        exact_logs(a_ref, b_ref, t_refs[0], l_ref)


def by_coordinates(v, p):
    hi, lo = halves(p)
    return jnp.dot(v, hi, preferred_element_type=F32) + jnp.dot(v, lo, preferred_element_type=F32)


def weighted(a_ref, b_ref, v_ref, t_refs, o_ref):
    def use(t_ref, rows, cols):
        part = by_coordinates(v_ref[:, rows], jnp.exp2(t_ref[...]))
        o_ref[:, cols] = part if rows.start == 0 else o_ref[:, cols] + part

    blocks(a_ref, b_ref, t_refs, 0, use)


def row_logs(x_hbm, y_hbm, g_hbm, out_ref, x_ref, y_ref, g_ref, a_ref, b_ref, l_ref, t0_ref, t1_ref, sems):
    t_refs = (t0_ref, t1_ref)
    sides = ((y_hbm, y_ref), (x_hbm, x_ref), (g_hbm, g_ref))
    copies = [pltpu.make_async_copy(*pair, sems.at[i]) for i, pair in enumerate(sides)]
    for copy in copies:
        copy.start()
    for copy in copies:
        copy.wait()
    x, y = x_ref[...], y_ref[...]
    y_sq = jnp.sum(y * y, 0, keepdims=True)
    lift = (g_ref[...] - y_sq) * C2
    longest = jnp.sqrt(jnp.sum(x * x, 0, keepdims=True)) * jnp.sqrt(jnp.max(y_sq, 1, keepdims=True))
    bound = jnp.max(lift, 1, keepdims=True) + 2 * C2 * longest
    a_ref[...] = first_side(y, lift).T
    b_ref[...] = second_side(x * (2 * C2), -bound)
    log_sums(a_ref, b_ref, t_refs, l_ref)
    total = l_ref[...] + bound
    for k in range(out_ref.shape[1]):
        for d in range(out_ref.shape[0]):
            out_ref[d, k : k + 1, :] = cut(total, k)


def core_of(me_ref):
    return me_ref[0] >> 3 & 1


def side_of(me_ref):
    return me_ref[0] >> 2 & 1


def column_sums(log_n, first, me_ref, x_ref, y_ref, g_ref, from_ref, *refs):
    if first:
        pot_ref, total_ref, out_ref, a_ref, b_ref, v_ref, o_ref, l_ref, *t_refs = refs
        parts = from_ref[...]
        top = jnp.max(parts, 0)
        total = top + jnp.log2(jnp.sum(jnp.exp2(parts - top[None]), 0))
        total = jnp.concatenate([total[k : k + 1, :] for k in range(total.shape[0])], 1) + log_n
        total_ref[...] = total
        pot_ref[...] = jnp.sum(x_ref[...] * x_ref[...], 0, keepdims=True) - LN * total
    else:
        out_ref, a_ref, b_ref, v_ref, o_ref, l_ref, *t_refs = refs
        total = from_ref[...]
    half = o_ref.shape[1]
    side = 1 - core_of(me_ref) if first else core_of(me_ref)
    cols = pl.ds(pl.multiple_of(side * half, half), half)
    x, y = x_ref[...], y_ref[:, cols]
    bound = (jnp.sum(y * y, 0, keepdims=True) - g_ref[:, cols]) * C2 - log_n
    a_ref[...] = first_side(x * (2 * C2), -total).T
    b_ref[...] = second_side(y, -bound)
    v_ref[...] = coordinates(x)
    weighted(a_ref, b_ref, v_ref, t_refs, o_ref)
    mass = o_ref[2 * K : 2 * K + 1, :]
    l_ref[...] = jnp.log2(mass) + bound

    @pl.when(jnp.min(mass) < LEAST)
    def _():
        t_ref = t_refs[0]
        wide = t_ref.shape[1]
        exact_logs(a_ref, b_ref, t_ref, l_ref)
        l_ref[...] += bound
        b_ref[6 * K : KD, :] = offsets(-l_ref[...], False)

        def column(c, _):
            at = pl.ds(pl.multiple_of(c * wide, wide), wide)
            t_ref[...] = jnp.dot(a_ref[...], b_ref[:, at], preferred_element_type=F32)
            o_ref[:, at] = by_coordinates(v_ref[...], jnp.exp2(t_ref[...]))
            return 0

        lax.fori_loop(0, half // wide, column, 0)

    for q in range(out_ref.shape[0]):
        at = slice(q * LANES, (q + 1) * LANES)
        out_ref[q, 0:K, :] = (o_ref[0:K, at] + o_ref[K : 2 * K, at]) / o_ref[2 * K : 2 * K + 1, at]
        out_ref[q, K : K + 8, :] = jnp.broadcast_to(l_ref[:, at], (8, LANES))


def merge(logs, images):
    top = functools.reduce(jnp.maximum, logs)
    shares = [jnp.exp2(one - top) for one in logs]
    mass = functools.reduce(jnp.add, shares)
    image = functools.reduce(jnp.add, [w * i for w, i in zip(shares, images)])
    return top + jnp.log2(mass), image / mass


def merge_pair(one_ref, two_ref, out_ref):
    pair, n = (one_ref, two_ref), out_ref.shape[0]
    log, image = merge([ref[:, K : K + 8, :][:, 0:1, :] for ref in pair], [ref[:, 0:K, :] for ref in pair])
    out_ref[:, 0:K, :] = image
    for q in range(n):
        out_ref[0, K + q : K + q + 1, :] = log[q]
    for d in range(1, n):
        out_ref[d, K:, :] = out_ref[0, K:, :]


def merge_logs(part_ref, out_ref):
    parts = [part_ref[d, K:, :] for d in range(part_ref.shape[0])]
    top = functools.reduce(jnp.maximum, parts)
    out_ref[...] = top + jnp.log2(functools.reduce(jnp.add, [jnp.exp2(part - top) for part in parts]))


def merge_chunk(me_ref, part_ref, after_ref, out_ref):
    n = part_ref.shape[0]
    logs = [part_ref[d, pl.ds(K + (me_ref[0] >> 4), 1), :] for d in range(n)]
    _, image = merge(logs, [part_ref[d, 0:K, :] for d in range(n)])
    for d in range(n):
        out_ref[d] = image


def row_images(log_n, own, me_ref, x_ref, y_ref, total_ref, mine_ref, other_ref, after_ref, pot_ref, out_ref, a_ref, b_ref, v_ref, o_ref, l_ref, *t_refs):
    for part, ref in ((core_of(me_ref), mine_ref), (1 - core_of(me_ref), other_ref)):
        for q in range(ref.shape[0]):
            at = pl.ds(pl.multiple_of((part * ref.shape[0] + q) * LANES, LANES), LANES)
            l_ref[:, at] = ref[q : q + 1, :]
    logs = l_ref[...]
    y = y_ref[...]
    pot_ref[...] = jnp.sum(y * y, 0, keepdims=True) - LN * (logs + log_n)
    half = o_ref.shape[1]
    side = side_of(me_ref) if own else 1 - side_of(me_ref)
    cols = pl.ds(pl.multiple_of(side * half, half), half)
    a_ref[...] = first_side(y, -logs).T
    b_ref[...] = second_side(x_ref[:, cols] * (2 * C2), LIFT - total_ref[:, cols])
    v_ref[...] = coordinates(y)
    weighted(a_ref, b_ref, v_ref, t_refs, o_ref)
    tiles = half // LANES
    for k in range(tiles):
        lanes = slice(k * LANES, (k + 1) * LANES)
        for r in range(0, K, 8):
            out_ref[r * tiles + 8 * k : r * tiles + 8 * k + 8, :] = o_ref[r : r + 8, lanes] + o_ref[K + r : K + r + 8, lanes]
        out_ref[K * tiles + k : K * tiles + k + 1, :] = o_ref[2 * K : 2 * K + 1, lanes]
    out_ref[K * tiles + tiles :, :] = jnp.ones((out_ref.shape[0] - (K + 1) * tiles, LANES), F32)


def add_divide(one_ref, two_ref, out_ref):
    rows = out_ref.shape[0]
    tiles = rows // K
    mass = one_ref[rows : rows + 8, :] + two_ref[rows : rows + 8, :]
    for k in range(tiles):
        under = jnp.broadcast_to(mass[k : k + 1, :], (8, LANES))
        for r in range(0, K, 8):
            at = slice(r * tiles + 8 * k, r * tiles + 8 * k + 8)
            out_ref[at, :] = (one_ref[at, :] + two_ref[at, :]) / under


def lay_rows(me_ref, mine_ref, other_ref, out_ref):
    half = out_ref.shape[1] // 2
    tiles = half // LANES
    for side, ref in ((side_of(me_ref), mine_ref), (1 - side_of(me_ref), other_ref)):
        for k in range(tiles):
            cols = pl.ds(pl.multiple_of(side * half + k * LANES, LANES), LANES)
            for r in range(0, K, 8):
                out_ref[r : r + 8, cols] = ref[r * tiles + 8 * k : r * tiles + 8 * k + 8, :]


def hold(image_ref, after_ref, out_ref):
    pass


def lay_columns(me_ref, mine_ref, other_ref, out_ref):
    half = out_ref.shape[1] // 2
    for side, ref in ((core_of(me_ref), mine_ref), (1 - core_of(me_ref), other_ref)):
        for q in range(ref.shape[0]):
            out_ref[:, pl.ds(pl.multiple_of(side * half + q * LANES, LANES), LANES)] = ref[q]


def call(kernel, ins, outs, scratch=(), copies=0, aliases={}, cost=None):
    return pl.pallas_call(
        kernel,
        out_shape=tuple(jax.ShapeDtypeStruct(shape, F32) for shape in outs),
        in_specs=[{"s": SM, "h": pl.BlockSpec(memory_space=pltpu.HBM), "v": VM}[spec] for spec in ins],
        out_specs=tuple(VM for _ in outs),
        scratch_shapes=[pltpu.VMEM(*one) for one in scratch] + [pltpu.SemaphoreType.DMA((copies,))] * (copies > 0),
        input_output_aliases=aliases,
        cost_estimate=cost,
        compiler_params=pltpu.CompilerParams(vmem_limit_bytes=50 << 20),
    )


def work(pairs, sums):
    return pl.CostEstimate(flops=2 * pairs * (KD + 256 * sums), transcendentals=pairs, bytes_accessed=8 * pairs)


def solution(mesh):
    n_src, n_tgt = mesh.shape["src"], mesh.shape["tgt"]
    pairs, ring = n_src // 2, n_tgt // 2
    grid = Mesh(mesh.devices.reshape(2, pairs // 2, 2, 2, ring), ("high", "line", "core", "low", "ring"))
    chips, tgt = ("high", "line"), ("low", "ring")
    src = (*chips, "core")
    swap = [(0, 1), (1, 0)]
    over = [(i, (i + ring) % n_tgt) for i in range(n_tgt)]
    near = [(i, i ^ 1) for i in range(n_tgt)]
    far = [(i, i ^ 3) for i in range(n_tgt)]

    def shards(x, y, g):
        ns, nt = x.shape[1], y.shape[1]
        rows = ns // LANES
        me = lax.axis_index(src + tgt).astype(jnp.int32).reshape(1)
        g = g.reshape(1, nt)
        chunk = (pairs, K + 8, LANES)

        part, x, y, g = call(
            row_logs,
            "hhh",
            [(n_tgt, rows, LANES), x.shape, y.shape, g.shape],
            [((nt, KD), BF), ((KD, ns), BF), ((1, ns), F32), BLOCK, BLOCK],
            3,
            cost=work(ns * nt, 0),
        )(*(pltpu.with_memory_space_constraint(one, pltpu.HBM) for one in (x, y, g)))
        part = lax.all_to_all(part, tgt, 0, 0, tiled=True)

        sums = [((ns, KD), BF), ((KD, nt // 2), BF), ((80, ns), BF), ((80, nt // 2), F32), ((1, nt // 2), F32), BLOCK, BLOCK]
        log_n = math.log2(ns * n_src)
        source_potential, total, send = call(
            functools.partial(column_sums, log_n, True), "svvvv", [(1, ns), (1, ns), chunk], sums, cost=work(ns * nt // 2, 2)
        )(me, x, y, g, part)
        sent = lax.ppermute(send, "core", swap)
        (keep,) = call(
            functools.partial(column_sums, log_n, False), "svvvv", [chunk], sums, cost=work(ns * nt // 2, 2)
        )(me, x, y, g, total)
        (part,) = call(merge_pair, "vv", [(pairs, K + pairs, LANES)])(keep, sent)
        image = lax.all_to_all(part, chips, 0, 0, tiled=True)
        (mine,) = call(merge_logs, "v", [(pairs, LANES)])(image)
        other = lax.ppermute(mine, "core", swap)

        half = ns // 2
        tall = (K * half) // LANES
        images = lambda own: call(
            functools.partial(row_images, math.log2(nt * n_tgt), own),
            "svvvvvv",
            [(1, nt), (tall + 8, LANES)],
            [((nt, KD), BF), ((KD, half), BF), ((80, nt), BF), ((80, half), F32), ((1, nt), F32), BLOCK, BLOCK],
            cost=work(half * nt, 2),
        )
        target_potential, sent = images(False)(me, x, y, total, mine, other, mine)
        _, held = images(True)(me, x, y, total, mine, other, sent)
        sent = lax.ppermute(sent, tgt, over)
        held = held + sent
        (image,) = call(merge_chunk, "svv", [(pairs, K, LANES)], cost=work(half * nt, 2))(me, image, held)
        image = lax.all_to_all(image, chips, 0, 0, tiled=True)
        held = held + lax.ppermute(held, tgt, near)
        (held,) = call(add_divide, "vv", [(tall, LANES)], cost=work(half * nt, 2))(held, lax.ppermute(held, tgt, far))
        sent = lax.ppermute(held, tgt, over)
        (source_image,) = call(lay_rows, "svv", [(K, ns)], cost=work(half * nt, 2))(me, held, sent)
        (image,) = call(hold, "vv", [image.shape], aliases={0: 0})(image, sent)
        (target_image,) = call(lay_columns, "svv", [(K, nt)])(me, image, lax.ppermute(image, "core", swap))
        return source_potential.reshape(ns), target_potential.reshape(nt), source_image, target_image

    return jax.shard_map(
        shards,
        mesh=grid,
        in_specs=(P(None, src), P(None, tgt), P(tgt)),
        out_specs=(P(src), P(tgt), P(None, src), P(None, tgt)),
        check_vma=False,
    )
```

```python
import functools
import math

import jax
import jax.numpy as jnp
from jax import lax
from jax.experimental import pallas as pl
from jax.experimental.pallas import tpu as pltpu
from jax.sharding import Mesh
from jax.sharding import PartitionSpec as P

EPS = 0.05
C2 = 1.4426950408889634 / EPS
LN = EPS * math.log(2.0)
LEAST = 2.0**-80
LIFT = 64.0
BF = jnp.bfloat16
F32 = jnp.float32
K = 32
KD = 8 * K
VM = pl.BlockSpec(memory_space=pltpu.VMEM)
SM = pl.BlockSpec(memory_space=pltpu.SMEM)
LANES = 128
TALL, WIDE = 1024, 512
BLOCK = ((TALL, WIDE), F32)


def thirds(v):
    hi = v.astype(BF)
    rest = v - hi.astype(F32)
    mid = rest.astype(BF)
    return hi, mid, (rest - mid.astype(F32)).astype(BF)


def halves(v):
    hi = v.astype(BF)
    return hi, (v - hi.astype(F32)).astype(BF)


def offsets(b, first):
    hi, mid, lo = (part.astype(F32) for part in thirds(b))
    row = lax.broadcasted_iota(jnp.int32, (2 * K, b.shape[1]), 0)
    row, one = (row, row - 3) if first else (row - 3, row)
    value = jnp.where(row == 0, hi, jnp.where(row == 1, mid, jnp.where(row == 2, lo, 0.0)))
    return jnp.where((one >= 0) & (one < 3), 1.0, value).astype(BF)


def first_side(v, b):
    hi, mid, lo = thirds(v)
    return jnp.concatenate([hi, hi, hi, mid, mid, lo, offsets(b, True)], 0)


def second_side(v, b):
    hi, mid, lo = thirds(v)
    return jnp.concatenate([hi, mid, lo, hi, mid, hi, offsets(b, False)], 0)


def coordinates(v):
    hi, lo = halves(v)
    return jnp.concatenate([hi, lo, jnp.ones((K // 2, v.shape[1]), BF)], 0)


def cut(tiles, k):
    return tiles[:, k * LANES : (k + 1) * LANES]


def blocks(a_ref, b_ref, t_refs, first, use):
    tall, wide = t_refs[0].shape
    places = [(r, c) for c in range(first, first + b_ref.shape[1], wide) for r in range(0, a_ref.shape[0], tall)]

    def fill(i):
        r, c = places[i]
        t_refs[i % 2][...] = jnp.dot(a_ref[r : r + tall, :], b_ref[:, c : c + wide], preferred_element_type=F32)

    fill(0)
    for i, (r, c) in enumerate(places):
        if i + 1 < len(places):
            fill(i + 1)
        use(t_refs[i % 2], slice(r, r + tall), slice(c, c + wide))


def exact_logs(a_ref, b_ref, t_ref, l_ref):
    tall, wide = t_ref.shape

    def column(c, _):
        cols = pl.ds(pl.multiple_of(c * wide, wide), wide)

        def fill(r):
            rows = pl.ds(pl.multiple_of(r * tall, tall), tall)
            t_ref[...] = jnp.dot(a_ref[rows, :], b_ref[:, cols], preferred_element_type=F32)

        def highest(r, peak):
            fill(r)
            return jnp.maximum(peak, jnp.max(t_ref[...], 0, keepdims=True))

        count = a_ref.shape[0] // tall
        peak = lax.fori_loop(0, count, highest, jnp.full((1, wide), -1e30, F32))

        def add(r, total):
            fill(r)
            return total + jnp.sum(jnp.exp2(t_ref[...] - peak), 0, keepdims=True)

        l_ref[:, cols] = peak + jnp.log2(lax.fori_loop(0, count, add, jnp.zeros((1, wide), F32)))
        return 0

    lax.fori_loop(0, b_ref.shape[1] // wide, column, 0)


def log_sums(a_ref, b_ref, t_refs, l_ref):
    def use(t_ref, rows, cols):
        part = jnp.sum(jnp.exp2(t_ref[...]), 0, keepdims=True)
        l_ref[:, cols] = part if rows.start == 0 else l_ref[:, cols] + part

    blocks(a_ref, b_ref, t_refs, 0, use)
    least = jnp.min(l_ref[...])
    l_ref[...] = jnp.log2(l_ref[...])

    @pl.when(least < LEAST)
    def _():
        exact_logs(a_ref, b_ref, t_refs[0], l_ref)


def by_coordinates(v, p):
    hi, lo = halves(p)
    return jnp.dot(v, hi, preferred_element_type=F32) + jnp.dot(v, lo, preferred_element_type=F32)


def weighted(a_ref, b_ref, v_ref, t_refs, o_ref):
    def use(t_ref, rows, cols):
        part = by_coordinates(v_ref[:, rows], jnp.exp2(t_ref[...]))
        o_ref[:, cols] = part if rows.start == 0 else o_ref[:, cols] + part

    blocks(a_ref, b_ref, t_refs, 0, use)


def row_logs(me_ref, x_hbm, y_hbm, g_hbm, out_ref, x_ref, y_ref, g_ref, a_ref, b_ref, l_ref, t0_ref, t1_ref, sems):
    t_refs = (t0_ref, t1_ref)
    sides = ((y_hbm, y_ref), (x_hbm, x_ref), (g_hbm, g_ref))
    copies = [pltpu.make_async_copy(*pair, sems.at[i]) for i, pair in enumerate(sides)]
    for copy in copies:
        copy.start()
    for copy in copies:
        copy.wait()
    x, y = x_ref[...], y_ref[...]
    y_sq = jnp.sum(y * y, 0, keepdims=True)
    lift = (g_ref[...] - y_sq) * C2
    longest = jnp.sqrt(jnp.sum(x * x, 0, keepdims=True)) * jnp.sqrt(jnp.max(y_sq, 1, keepdims=True))
    bound = jnp.max(lift, 1, keepdims=True) + 2 * C2 * longest
    a_ref[...] = first_side(y, lift).T
    b_ref[...] = second_side(x * (2 * C2), -bound)
    log_sums(a_ref, b_ref, t_refs, l_ref)
    total = l_ref[...] + bound
    for k in range(out_ref.shape[1]):
        for d in range(out_ref.shape[0]):
            out_ref[d, k : k + 1, :] = cut(total, k)


def core_of(me_ref):
    return me_ref[0] >> 3 & 1


def side_of(me_ref):
    return me_ref[0] >> 2 & 1


def column_sums(log_n, first, me_ref, x_ref, y_ref, g_ref, from_ref, *refs):
    if first:
        pot_ref, total_ref, out_ref, a_ref, v_ref, b_ref, o_ref, l_ref, *t_refs = refs
        parts = from_ref[...]
        top = jnp.max(parts, 0)
        total = top + jnp.log2(jnp.sum(jnp.exp2(parts - top[None]), 0))
        total = jnp.concatenate([total[k : k + 1, :] for k in range(total.shape[0])], 1) + log_n
        total_ref[...] = total
        x = x_ref[...]
        pot_ref[...] = jnp.sum(x * x, 0, keepdims=True) - LN * total
        a_ref[...] = first_side(x * (2 * C2), -total).T
        v_ref[...] = coordinates(x)
    else:
        a_ref, v_ref, out_ref, b_ref, o_ref, l_ref, *t_refs = refs
    half = o_ref.shape[1]
    side = 1 - core_of(me_ref) if first else core_of(me_ref)
    cols = pl.ds(pl.multiple_of(side * half, half), half)
    y = y_ref[:, cols]
    bound = (jnp.sum(y * y, 0, keepdims=True) - g_ref[:, cols]) * C2 - log_n
    b_ref[...] = second_side(y, -bound)
    weighted(a_ref, b_ref, v_ref, t_refs, o_ref)
    mass = o_ref[2 * K : 2 * K + 1, :]
    l_ref[...] = jnp.log2(mass) + bound

    @pl.when(jnp.min(mass) < LEAST)
    def _():
        t_ref = t_refs[0]
        wide = t_ref.shape[1]
        exact_logs(a_ref, b_ref, t_ref, l_ref)
        l_ref[...] += bound
        b_ref[6 * K : KD, :] = offsets(-l_ref[...], False)

        def column(c, _):
            at = pl.ds(pl.multiple_of(c * wide, wide), wide)
            t_ref[...] = jnp.dot(a_ref[...], b_ref[:, at], preferred_element_type=F32)
            o_ref[:, at] = by_coordinates(v_ref[...], jnp.exp2(t_ref[...]))
            return 0

        lax.fori_loop(0, half // wide, column, 0)

    for q in range(out_ref.shape[0]):
        at = slice(q * LANES, (q + 1) * LANES)
        out_ref[q, 0:K, :] = (o_ref[0:K, at] + o_ref[K : 2 * K, at]) / o_ref[2 * K : 2 * K + 1, at]
        out_ref[q, K : K + 8, :] = jnp.broadcast_to(l_ref[:, at], (8, LANES))


def merge(logs, images):
    top = functools.reduce(jnp.maximum, logs)
    shares = [jnp.exp2(one - top) for one in logs]
    mass = functools.reduce(jnp.add, shares)
    image = functools.reduce(jnp.add, [w * i for w, i in zip(shares, images)])
    return top + jnp.log2(mass), image / mass


def merge_pair(one_ref, two_ref, out_ref):
    pair, n = (one_ref, two_ref), out_ref.shape[0]
    log, image = merge([ref[:, K : K + 8, :][:, 0:1, :] for ref in pair], [ref[:, 0:K, :] for ref in pair])
    out_ref[:, 0:K, :] = image
    for q in range(n):
        out_ref[0, K + q : K + q + 1, :] = log[q]
    for d in range(1, n):
        out_ref[d, K:, :] = out_ref[0, K:, :]


def merge_logs(part_ref, out_ref):
    parts = [part_ref[d, K:, :] for d in range(part_ref.shape[0])]
    top = functools.reduce(jnp.maximum, parts)
    out_ref[...] = top + jnp.log2(functools.reduce(jnp.add, [jnp.exp2(part - top) for part in parts]))


def merge_chunk(me_ref, part_ref, after_ref, out_ref):
    n = part_ref.shape[0]
    logs = [part_ref[d, pl.ds(K + (me_ref[0] >> 4), 1), :] for d in range(n)]
    _, image = merge(logs, [part_ref[d, 0:K, :] for d in range(n)])
    for d in range(n):
        out_ref[d] = image


def row_sides(log_n, me_ref, y_ref, mine_ref, other_ref, pot_ref, a_ref, v_ref, l_ref):
    for part, ref in ((core_of(me_ref), mine_ref), (1 - core_of(me_ref), other_ref)):
        for q in range(ref.shape[0]):
            at = pl.ds(pl.multiple_of((part * ref.shape[0] + q) * LANES, LANES), LANES)
            l_ref[:, at] = ref[q : q + 1, :]
    logs = l_ref[...]
    y = y_ref[...]
    pot_ref[...] = jnp.sum(y * y, 0, keepdims=True) - LN * (logs + log_n)
    a_ref[...] = first_side(y, -logs).T
    v_ref[...] = coordinates(y)


def row_images(log_n, own, me_ref, x_ref, total_ref, after_ref, *refs):
    if own:
        a_ref, v_ref, out_ref, b_ref, o_ref, *t_refs = refs
    else:
        y_ref, mine_ref, other_ref, pot_ref, out_ref, a_ref, v_ref, b_ref, o_ref, l_ref, *t_refs = refs
        row_sides(log_n, me_ref, y_ref, mine_ref, other_ref, pot_ref, a_ref, v_ref, l_ref)
    half = o_ref.shape[1]
    side = side_of(me_ref) if own else 1 - side_of(me_ref)
    cols = pl.ds(pl.multiple_of(side * half, half), half)
    b_ref[...] = second_side(x_ref[:, cols] * (2 * C2), LIFT - total_ref[:, cols])
    weighted(a_ref, b_ref, v_ref, t_refs, o_ref)
    tiles = half // LANES
    for k in range(tiles):
        lanes = slice(k * LANES, (k + 1) * LANES)
        for r in range(0, K, 8):
            out_ref[r * tiles + 8 * k : r * tiles + 8 * k + 8, :] = o_ref[r : r + 8, lanes] + o_ref[K + r : K + r + 8, lanes]
        out_ref[K * tiles + k : K * tiles + k + 1, :] = o_ref[2 * K : 2 * K + 1, lanes]
    out_ref[K * tiles + tiles :, :] = jnp.ones((out_ref.shape[0] - (K + 1) * tiles, LANES), F32)


def add_divide(one_ref, two_ref, out_ref):
    rows = out_ref.shape[0]
    tiles = rows // K
    mass = one_ref[rows : rows + 8, :] + two_ref[rows : rows + 8, :]
    for k in range(tiles):
        under = jnp.broadcast_to(mass[k : k + 1, :], (8, LANES))
        for r in range(0, K, 8):
            at = slice(r * tiles + 8 * k, r * tiles + 8 * k + 8)
            out_ref[at, :] = (one_ref[at, :] + two_ref[at, :]) / under


def lay_rows(me_ref, mine_ref, other_ref, out_ref, token_ref):
    token_ref[...] = mine_ref[0:8, :]
    half = out_ref.shape[1] // 2
    tiles = half // LANES
    for side, ref in ((side_of(me_ref), mine_ref), (1 - side_of(me_ref), other_ref)):
        for k in range(tiles):
            cols = pl.ds(pl.multiple_of(side * half + k * LANES, LANES), LANES)
            for r in range(0, K, 8):
                out_ref[r : r + 8, cols] = ref[r * tiles + 8 * k : r * tiles + 8 * k + 8, :]


def hold(image_ref, after_ref, out_ref):
    pass


def lay_columns(me_ref, mine_ref, other_ref, out_ref):
    half = out_ref.shape[1] // 2
    for side, ref in ((core_of(me_ref), mine_ref), (1 - core_of(me_ref), other_ref)):
        for q in range(ref.shape[0]):
            out_ref[:, pl.ds(pl.multiple_of(side * half + q * LANES, LANES), LANES)] = ref[q]


def call(kernel, ins, outs, scratch=(), copies=0, aliases={}, cost=None, out="v"):
    spaces = {"s": SM, "h": pl.BlockSpec(memory_space=pltpu.HBM), "v": VM}
    return pl.pallas_call(
        kernel,
        out_shape=tuple(jax.ShapeDtypeStruct(*(one if isinstance(one[0], tuple) else (one, F32))) for one in outs),
        in_specs=[spaces[spec] for spec in ins],
        out_specs=tuple(spaces[out] for _ in outs),
        scratch_shapes=[pltpu.VMEM(*one) for one in scratch] + [pltpu.SemaphoreType.DMA((copies,))] * (copies > 0),
        input_output_aliases=aliases,
        cost_estimate=cost,
        compiler_params=pltpu.CompilerParams(vmem_limit_bytes=50 << 20),
    )


def work(pairs, sums):
    return pl.CostEstimate(flops=2 * pairs * (KD + 256 * sums), transcendentals=pairs, bytes_accessed=8 * pairs)


def solution(mesh):
    n_src, n_tgt = mesh.shape["src"], mesh.shape["tgt"]
    pairs, ring = n_src // 2, n_tgt // 2
    grid = Mesh(mesh.devices.reshape(2, pairs // 2, 2, 2, ring), ("high", "line", "core", "low", "ring"))
    chips, tgt = ("high", "line"), ("low", "ring")
    src = (*chips, "core")
    swap = [(0, 1), (1, 0)]
    over = [(i, (i + ring) % n_tgt) for i in range(n_tgt)]
    near = [(i, i ^ 1) for i in range(n_tgt)]
    far = [(i, i ^ 3) for i in range(n_tgt)]

    def shards(x, y, g):
        ns, nt = x.shape[1], y.shape[1]
        rows = ns // LANES
        me = lax.axis_index(src + tgt).astype(jnp.int32).reshape(1)
        g = g.reshape(1, nt)
        chunk = (pairs, K + 8, LANES)

        part, x, y, g = call(
            row_logs,
            "shhh",
            [(n_tgt, rows, LANES), x.shape, y.shape, g.shape],
            [((nt, KD), BF), ((KD, ns), BF), ((1, ns), F32), BLOCK, BLOCK],
            3,
            cost=work(ns * nt, 0),
        )(me, *(pltpu.with_memory_space_constraint(one, pltpu.HBM) for one in (x, y, g)))
        part = lax.all_to_all(part, tgt, 0, 0, tiled=True)

        sums = [((KD, nt // 2), BF), ((80, nt // 2), F32), ((1, nt // 2), F32), BLOCK, BLOCK]
        log_n = math.log2(ns * n_src)
        source_potential, total, send, side, weights = call(
            functools.partial(column_sums, log_n, True),
            "svvvv",
            [(1, ns), (1, ns), chunk, ((ns, KD), BF), ((80, ns), BF)],
            sums,
            cost=work(ns * nt // 2, 2),
        )(me, x, y, g, part)
        sent = lax.ppermute(send, "core", swap)
        (keep,) = call(
            functools.partial(column_sums, log_n, False), "svvvvvv", [chunk], sums, cost=work(ns * nt // 2, 2)
        )(me, x, y, g, total, side, weights)
        (part,) = call(merge_pair, "vv", [(pairs, K + pairs, LANES)])(keep, sent)
        image = lax.all_to_all(part, chips, 0, 0, tiled=True)
        (mine,) = call(merge_logs, "v", [(pairs, LANES)])(image)
        other = lax.ppermute(mine, "core", swap)

        (image,) = call(merge_chunk, "svv", [(pairs, K, LANES)], cost=work(ns * nt // 2, 2))(me, image, mine)

        half = ns // 2
        tall = (K * half) // LANES
        sums = [((KD, half), BF), ((80, half), F32)]
        log_n = math.log2(nt * n_tgt)
        target_potential, sent, side, weights = call(
            functools.partial(row_images, log_n, False),
            "svvhvvv",
            [(1, nt), (tall + 8, LANES), ((nt, KD), BF), ((80, nt), BF)],
            [*sums, ((1, nt), F32), BLOCK, BLOCK],
            cost=work(half * nt, 2),
        )(me, x, total, image, y, mine, other)
        (held,) = call(
            functools.partial(row_images, log_n, True),
            "svvvvv",
            [(tall + 8, LANES)],
            [*sums, BLOCK, BLOCK],
            cost=work(half * nt, 2),
        )(me, x, total, sent, side, weights)
        held = held + lax.ppermute(sent, tgt, over)
        (image,) = call(hold, "hv", [image.shape], aliases={0: 0}, out="h")(image, held)
        image = lax.all_to_all(image, chips, 0, 0, tiled=True)
        held = held + lax.ppermute(held, tgt, near)
        (held,) = call(add_divide, "vv", [(tall, LANES)], cost=work(half * nt, 2))(held, lax.ppermute(held, tgt, far))
        source_image, token = call(lay_rows, "svv", [(K, ns), (8, LANES)])(
            me, held, lax.ppermute(held, tgt, over)
        )
        (image,) = call(hold, "vv", [image.shape], aliases={0: 0})(image, token)
        (target_image,) = call(lay_columns, "svv", [(K, nt)])(me, image, lax.ppermute(image, "core", swap))
        return source_potential.reshape(ns), target_potential.reshape(nt), source_image, target_image

    return jax.shard_map(
        shards,
        mesh=grid,
        in_specs=(P(None, src), P(None, tgt), P(tgt)),
        out_specs=(P(src), P(tgt), P(None, src), P(None, tgt)),
        check_vma=False,
    )
```

```python
import functools
import math

import jax
import jax.numpy as jnp
from jax import lax
from jax.experimental import pallas as pl
from jax.experimental.pallas import tpu as pltpu
from jax.sharding import Mesh
from jax.sharding import PartitionSpec as P

EPS = 0.05
C2 = 1.4426950408889634 / EPS
LN = EPS * math.log(2.0)
LEAST = 2.0**-80
LIFT = 64.0
BF = jnp.bfloat16
F32 = jnp.float32
K = 32
KD = 8 * K
VM = pl.BlockSpec(memory_space=pltpu.VMEM)
SM = pl.BlockSpec(memory_space=pltpu.SMEM)
LANES = 128
TALL, WIDE = 1024, 512
BLOCK = ((TALL, WIDE), F32)


def thirds(v):
    hi = v.astype(BF)
    rest = v - hi.astype(F32)
    mid = rest.astype(BF)
    return hi, mid, (rest - mid.astype(F32)).astype(BF)


def halves(v):
    hi = v.astype(BF)
    return hi, (v - hi.astype(F32)).astype(BF)


def offsets(b, first):
    hi, mid, lo = (part.astype(F32) for part in thirds(b))
    row = lax.broadcasted_iota(jnp.int32, (2 * K, b.shape[1]), 0)
    row, one = (row, row - 3) if first else (row - 3, row)
    value = jnp.where(row == 0, hi, jnp.where(row == 1, mid, jnp.where(row == 2, lo, 0.0)))
    return jnp.where((one >= 0) & (one < 3), 1.0, value).astype(BF)


def first_side(v, b):
    hi, mid, lo = thirds(v)
    return jnp.concatenate([hi, hi, hi, mid, mid, lo, offsets(b, True)], 0)


def second_side(v, b):
    hi, mid, lo = thirds(v)
    return jnp.concatenate([hi, mid, lo, hi, mid, hi, offsets(b, False)], 0)


def coordinates(v):
    hi, lo = halves(v)
    return jnp.concatenate([hi, lo, jnp.ones((K // 2, v.shape[1]), BF)], 0)


def cut(tiles, k):
    return tiles[:, k * LANES : (k + 1) * LANES]


def blocks(a_ref, b_ref, t_refs, first, use):
    tall, wide = t_refs[0].shape
    places = [(r, c) for c in range(first, first + b_ref.shape[1], wide) for r in range(0, a_ref.shape[0], tall)]

    def fill(i):
        r, c = places[i]
        t_refs[i % 2][...] = jnp.dot(a_ref[r : r + tall, :], b_ref[:, c : c + wide], preferred_element_type=F32)

    fill(0)
    for i, (r, c) in enumerate(places):
        if i + 1 < len(places):
            fill(i + 1)
        use(t_refs[i % 2], slice(r, r + tall), slice(c, c + wide))


def exact_logs(a_ref, b_ref, t_ref, l_ref):
    tall, wide = t_ref.shape

    def column(c, _):
        cols = pl.ds(pl.multiple_of(c * wide, wide), wide)

        def fill(r):
            rows = pl.ds(pl.multiple_of(r * tall, tall), tall)
            t_ref[...] = jnp.dot(a_ref[rows, :], b_ref[:, cols], preferred_element_type=F32)

        def highest(r, peak):
            fill(r)
            return jnp.maximum(peak, jnp.max(t_ref[...], 0, keepdims=True))

        count = a_ref.shape[0] // tall
        peak = lax.fori_loop(0, count, highest, jnp.full((1, wide), -1e30, F32))

        def add(r, total):
            fill(r)
            return total + jnp.sum(jnp.exp2(t_ref[...] - peak), 0, keepdims=True)

        l_ref[:, cols] = peak + jnp.log2(lax.fori_loop(0, count, add, jnp.zeros((1, wide), F32)))
        return 0

    lax.fori_loop(0, b_ref.shape[1] // wide, column, 0)


def log_sums(a_ref, b_ref, t_refs, l_ref):
    def use(t_ref, rows, cols):
        part = jnp.sum(jnp.exp2(t_ref[...]), 0, keepdims=True)
        l_ref[:, cols] = part if rows.start == 0 else l_ref[:, cols] + part

    blocks(a_ref, b_ref, t_refs, 0, use)
    least = jnp.min(l_ref[...])
    l_ref[...] = jnp.log2(l_ref[...])

    @pl.when(least < LEAST)
    def _():
        exact_logs(a_ref, b_ref, t_refs[0], l_ref)


def by_coordinates(v, p):
    hi, lo = halves(p)
    return jnp.dot(v, hi, preferred_element_type=F32) + jnp.dot(v, lo, preferred_element_type=F32)


def weighted(a_ref, b_ref, v_ref, t_refs, o_ref):
    def use(t_ref, rows, cols):
        part = by_coordinates(v_ref[:, rows], jnp.exp2(t_ref[...]))
        o_ref[:, cols] = part if rows.start == 0 else o_ref[:, cols] + part

    blocks(a_ref, b_ref, t_refs, 0, use)


def row_logs(me_ref, x_hbm, y_hbm, g_hbm, out_ref, x_ref, y_ref, g_ref, a_ref, b_ref, l_ref, t0_ref, t1_ref, sems):
    t_refs = (t0_ref, t1_ref)
    sides = ((y_hbm, y_ref), (x_hbm, x_ref), (g_hbm, g_ref))
    copies = [pltpu.make_async_copy(*pair, sems.at[i]) for i, pair in enumerate(sides)]
    for copy in copies:
        copy.start()
    for copy in copies:
        copy.wait()
    x, y = x_ref[...], y_ref[...]
    y_sq = jnp.sum(y * y, 0, keepdims=True)
    lift = (g_ref[...] - y_sq) * C2
    longest = jnp.sqrt(jnp.sum(x * x, 0, keepdims=True)) * jnp.sqrt(jnp.max(y_sq, 1, keepdims=True))
    bound = jnp.max(lift, 1, keepdims=True) + 2 * C2 * longest
    a_ref[...] = first_side(y, lift).T
    b_ref[...] = second_side(x * (2 * C2), -bound)
    log_sums(a_ref, b_ref, t_refs, l_ref)
    total = l_ref[...] + bound
    for k in range(out_ref.shape[1]):
        for d in range(out_ref.shape[0]):
            out_ref[d, k : k + 1, :] = cut(total, k)


def core_of(me_ref):
    return me_ref[0] >> 3 & 1


def column_sums(log_n, first, me_ref, x_ref, y_ref, g_ref, from_ref, *refs):
    if first:
        pot_ref, total_ref, out_ref, a_ref, v_ref, b_ref, o_ref, l_ref, *t_refs = refs
        parts = from_ref[...]
        top = jnp.max(parts, 0)
        total = top + jnp.log2(jnp.sum(jnp.exp2(parts - top[None]), 0))
        total = jnp.concatenate([total[k : k + 1, :] for k in range(total.shape[0])], 1) + log_n
        total_ref[...] = total
        x = x_ref[...]
        pot_ref[...] = jnp.sum(x * x, 0, keepdims=True) - LN * total
        a_ref[...] = first_side(x * (2 * C2), -total).T
        v_ref[...] = coordinates(x)
    else:
        a_ref, v_ref, out_ref, b_ref, o_ref, l_ref, *t_refs = refs
    half = o_ref.shape[1]
    side = 1 - core_of(me_ref) if first else core_of(me_ref)
    cols = pl.ds(pl.multiple_of(side * half, half), half)
    y = y_ref[:, cols]
    bound = (jnp.sum(y * y, 0, keepdims=True) - g_ref[:, cols]) * C2 - log_n
    b_ref[...] = second_side(y, -bound)
    weighted(a_ref, b_ref, v_ref, t_refs, o_ref)
    mass = o_ref[2 * K : 2 * K + 1, :]
    l_ref[...] = jnp.log2(mass) + bound

    @pl.when(jnp.min(mass) < LEAST)
    def _():
        t_ref = t_refs[0]
        wide = t_ref.shape[1]
        exact_logs(a_ref, b_ref, t_ref, l_ref)
        l_ref[...] += bound
        b_ref[6 * K : KD, :] = offsets(-l_ref[...], False)

        def column(c, _):
            at = pl.ds(pl.multiple_of(c * wide, wide), wide)
            t_ref[...] = jnp.dot(a_ref[...], b_ref[:, at], preferred_element_type=F32)
            o_ref[:, at] = by_coordinates(v_ref[...], jnp.exp2(t_ref[...]))
            return 0

        lax.fori_loop(0, half // wide, column, 0)

    for q in range(out_ref.shape[0]):
        at = slice(q * LANES, (q + 1) * LANES)
        out_ref[q, 0:K, :] = (o_ref[0:K, at] + o_ref[K : 2 * K, at]) / o_ref[2 * K : 2 * K + 1, at]
        out_ref[q, K : K + 8, :] = jnp.broadcast_to(l_ref[:, at], (8, LANES))


def merge(logs, images):
    top = functools.reduce(jnp.maximum, logs)
    shares = [jnp.exp2(one - top) for one in logs]
    mass = functools.reduce(jnp.add, shares)
    image = functools.reduce(jnp.add, [w * i for w, i in zip(shares, images)])
    return top + jnp.log2(mass), image / mass


def merge_pair(one_ref, two_ref, out_ref):
    pair, n = (one_ref, two_ref), out_ref.shape[0]
    log, image = merge([ref[:, K : K + 8, :][:, 0:1, :] for ref in pair], [ref[:, 0:K, :] for ref in pair])
    out_ref[:, 0:K, :] = image
    for q in range(n):
        out_ref[0, K + q : K + q + 1, :] = log[q]
    for d in range(1, n):
        out_ref[d, K:, :] = out_ref[0, K:, :]


def merge_logs(part_ref, out_ref):
    parts = [part_ref[d, K:, :] for d in range(part_ref.shape[0])]
    top = functools.reduce(jnp.maximum, parts)
    out_ref[...] = top + jnp.log2(functools.reduce(jnp.add, [jnp.exp2(part - top) for part in parts]))


def merge_chunk(me_ref, part_ref, after_ref, out_ref):
    n = part_ref.shape[0]
    logs = [part_ref[d, pl.ds(K + (me_ref[0] >> 4), 1), :] for d in range(n)]
    _, image = merge(logs, [part_ref[d, 0:K, :] for d in range(n)])
    for d in range(n):
        out_ref[d] = image


def row_images(log_n, me_ref, x_ref, total_ref, after_ref, y_ref, mine_ref, other_ref, pot_ref, out_ref, a_ref, b_ref, v_ref, o_ref, l_ref, *t_refs):
    for part, ref in ((core_of(me_ref), mine_ref), (1 - core_of(me_ref), other_ref)):
        for q in range(ref.shape[0]):
            at = pl.ds(pl.multiple_of((part * ref.shape[0] + q) * LANES, LANES), LANES)
            l_ref[:, at] = ref[q : q + 1, :]
    logs = l_ref[...]
    y = y_ref[...]
    pot_ref[...] = jnp.sum(y * y, 0, keepdims=True) - LN * (logs + log_n)
    a_ref[...] = first_side(y, -logs).T
    b_ref[...] = second_side(x_ref[...] * (2 * C2), LIFT - total_ref[...])
    v_ref[...] = coordinates(y)
    weighted(a_ref, b_ref, v_ref, t_refs, o_ref)
    tiles = o_ref.shape[1] // LANES
    for k in range(tiles):
        lanes = slice(k * LANES, (k + 1) * LANES)
        for r in range(0, K, 8):
            out_ref[r * tiles + 8 * k : r * tiles + 8 * k + 8, :] = o_ref[r : r + 8, lanes] + o_ref[K + r : K + r + 8, lanes]
        out_ref[K * tiles + k : K * tiles + k + 1, :] = o_ref[2 * K : 2 * K + 1, lanes]


def add(one_ref, two_ref, out_ref):
    out_ref[...] = one_ref[...] + two_ref[...]


def add_divide(one_ref, two_ref, out_ref):
    tiles = out_ref.shape[1] // LANES
    mass = one_ref[K * tiles :, :] + two_ref[K * tiles :, :]
    for k in range(tiles):
        under = jnp.broadcast_to(mass[k : k + 1, :], (8, LANES))
        for r in range(0, K, 8):
            at = slice(r * tiles + 8 * k, r * tiles + 8 * k + 8)
            out_ref[r : r + 8, k * LANES : (k + 1) * LANES] = (one_ref[at, :] + two_ref[at, :]) / under


def hold(image_ref, after_ref, out_ref):
    pass


def lay_columns(me_ref, mine_ref, other_ref, out_ref):
    half = out_ref.shape[1] // 2
    for side, ref in ((core_of(me_ref), mine_ref), (1 - core_of(me_ref), other_ref)):
        for q in range(ref.shape[0]):
            out_ref[:, pl.ds(pl.multiple_of(side * half + q * LANES, LANES), LANES)] = ref[q]


def call(kernel, ins, outs, scratch=(), copies=0, aliases={}, cost=None, out="v"):
    spaces = {"s": SM, "h": pl.BlockSpec(memory_space=pltpu.HBM), "v": VM}
    return pl.pallas_call(
        kernel,
        out_shape=tuple(jax.ShapeDtypeStruct(*(one if isinstance(one[0], tuple) else (one, F32))) for one in outs),
        in_specs=[spaces[spec] for spec in ins],
        out_specs=tuple(spaces[out] for _ in outs),
        scratch_shapes=[pltpu.VMEM(*one) for one in scratch] + [pltpu.SemaphoreType.DMA((copies,))] * (copies > 0),
        input_output_aliases=aliases,
        cost_estimate=cost,
        compiler_params=pltpu.CompilerParams(vmem_limit_bytes=50 << 20),
    )


def work(pairs, sums):
    return pl.CostEstimate(flops=2 * pairs * (KD + 256 * sums), transcendentals=pairs, bytes_accessed=8 * pairs)


def solution(mesh):
    n_src, n_tgt = mesh.shape["src"], mesh.shape["tgt"]
    pairs, ring = n_src // 2, n_tgt // 2
    grid = Mesh(mesh.devices.reshape(2, pairs // 2, 2, 2, ring), ("high", "line", "core", "low", "ring"))
    chips, tgt = ("high", "line"), ("low", "ring")
    src = (*chips, "core")
    swap = [(0, 1), (1, 0)]
    over = [(i, (i + ring) % n_tgt) for i in range(n_tgt)]
    near = [(i, i ^ 1) for i in range(n_tgt)]
    far = [(i, i ^ 3) for i in range(n_tgt)]

    def shards(x, y, g):
        ns, nt = x.shape[1], y.shape[1]
        rows = ns // LANES
        me = lax.axis_index(src + tgt).astype(jnp.int32).reshape(1)
        g = g.reshape(1, nt)
        chunk = (pairs, K + 8, LANES)

        part, x, y, g = call(
            row_logs,
            "shhh",
            [(n_tgt, rows, LANES), x.shape, y.shape, g.shape],
            [((nt, KD), BF), ((KD, ns), BF), ((1, ns), F32), BLOCK, BLOCK],
            3,
            cost=work(ns * nt, 0),
        )(me, *(pltpu.with_memory_space_constraint(one, pltpu.HBM) for one in (x, y, g)))
        part = lax.all_to_all(part, tgt, 0, 0, tiled=True)

        sums = [((KD, nt // 2), BF), ((80, nt // 2), F32), ((1, nt // 2), F32), BLOCK, BLOCK]
        log_n = math.log2(ns * n_src)
        source_potential, total, send, side, weights = call(
            functools.partial(column_sums, log_n, True),
            "svvvv",
            [(1, ns), (1, ns), chunk, ((ns, KD), BF), ((80, ns), BF)],
            sums,
            cost=work(ns * nt // 2, 2),
        )(me, x, y, g, part)
        sent = lax.ppermute(send, "core", swap)
        (keep,) = call(
            functools.partial(column_sums, log_n, False), "svvvvvv", [chunk], sums, cost=work(ns * nt // 2, 2)
        )(me, x, y, g, total, side, weights)
        (part,) = call(merge_pair, "vv", [(pairs, K + pairs, LANES)])(keep, sent)
        image = lax.all_to_all(part, chips, 0, 0, tiled=True)
        (mine,) = call(merge_logs, "v", [(pairs, LANES)])(image)
        other = lax.ppermute(mine, "core", swap)

        (image,) = call(merge_chunk, "svv", [(pairs, K, LANES)], cost=work(ns * nt // 2, 2))(me, image, mine)

        tall = (K * ns) // LANES
        target_potential, held = call(
            functools.partial(row_images, math.log2(nt * n_tgt)),
            "svvhvvv",
            [(1, nt), (tall + rows, LANES)],
            [((nt, KD), BF), ((KD, ns), BF), ((80, nt), BF), ((80, ns), F32), ((1, nt), F32), BLOCK, BLOCK],
            cost=work(ns * nt, 2),
        )(me, x, total, image, y, mine, other)
        (image,) = call(hold, "hv", [image.shape], aliases={0: 0}, out="h")(image, held)
        image = lax.all_to_all(image, chips, 0, 0, tiled=True)
        sizes = [held.shape]
        (held,) = call(add, "vv", sizes, cost=work(ns * nt // 4, 2))(held, lax.ppermute(held, tgt, over))
        (held,) = call(add, "vv", sizes, cost=work(ns * nt // 4, 2))(held, lax.ppermute(held, tgt, near))
        (source_image,) = call(add_divide, "vv", [(K, ns)], cost=work(ns * nt // 4, 2))(
            held, lax.ppermute(held, tgt, far)
        )
        (image,) = call(hold, "vv", [image.shape], aliases={0: 0})(image, held)
        (target_image,) = call(lay_columns, "svv", [(K, nt)])(me, image, lax.ppermute(image, "core", swap))
        return source_potential.reshape(ns), target_potential.reshape(nt), source_image, target_image

    return jax.shard_map(
        shards,
        mesh=grid,
        in_specs=(P(None, src), P(None, tgt), P(tgt)),
        out_specs=(P(src), P(tgt), P(None, src), P(None, tgt)),
        check_vma=False,
    )
```

```python
import functools
import math

import jax
import jax.numpy as jnp
from jax import lax
from jax.experimental import pallas as pl
from jax.experimental.pallas import tpu as pltpu
from jax.sharding import Mesh
from jax.sharding import PartitionSpec as P

EPS = 0.05
C2 = 1.4426950408889634 / EPS
LN = EPS * math.log(2.0)
LEAST = 2.0**-80
LIFT = 64.0
BF = jnp.bfloat16
F32 = jnp.float32
K = 32
KD = 8 * K
VM = pl.BlockSpec(memory_space=pltpu.VMEM)
SM = pl.BlockSpec(memory_space=pltpu.SMEM)
LANES = 128
TALL, WIDE = 1024, 256
BLOCK = ((TALL, WIDE), F32)


def thirds(v):
    hi = v.astype(BF)
    rest = v - hi.astype(F32)
    mid = rest.astype(BF)
    return hi, mid, (rest - mid.astype(F32)).astype(BF)


def halves(v):
    hi = v.astype(BF)
    return hi, (v - hi.astype(F32)).astype(BF)


def offsets(b, first):
    hi, mid, lo = (part.astype(F32) for part in thirds(b))
    row = lax.broadcasted_iota(jnp.int32, (2 * K, b.shape[1]), 0)
    row, one = (row, row - 3) if first else (row - 3, row)
    value = jnp.where(row == 0, hi, jnp.where(row == 1, mid, jnp.where(row == 2, lo, 0.0)))
    return jnp.where((one >= 0) & (one < 3), 1.0, value).astype(BF)


def first_side(v, b):
    hi, mid, lo = thirds(v)
    return jnp.concatenate([hi, hi, hi, mid, mid, lo, offsets(b, True)], 0)


def second_side(v, b):
    hi, mid, lo = thirds(v)
    return jnp.concatenate([hi, mid, lo, hi, mid, hi, offsets(b, False)], 0)


def coordinates(v):
    hi, lo = halves(v)
    return jnp.concatenate([hi, lo, jnp.ones((K // 2, v.shape[1]), BF)], 0)


def cut(tiles, k):
    return tiles[:, k * LANES : (k + 1) * LANES]


def blocks(a_ref, b_ref, t_refs, first, use):
    tall, wide = t_refs[0].shape
    places = [(r, c) for c in range(first, first + b_ref.shape[1], wide) for r in range(0, a_ref.shape[0], tall)]

    def fill(i):
        r, c = places[i]
        t_refs[i % 2][...] = jnp.dot(a_ref[r : r + tall, :], b_ref[:, c : c + wide], preferred_element_type=F32)

    fill(0)
    for i, (r, c) in enumerate(places):
        if i + 1 < len(places):
            fill(i + 1)
        use(t_refs[i % 2], slice(r, r + tall), slice(c, c + wide))


def exact_logs(a_ref, b_ref, t_ref, l_ref):
    tall, wide = t_ref.shape

    def column(c, _):
        cols = pl.ds(pl.multiple_of(c * wide, wide), wide)

        def fill(r):
            rows = pl.ds(pl.multiple_of(r * tall, tall), tall)
            t_ref[...] = jnp.dot(a_ref[rows, :], b_ref[:, cols], preferred_element_type=F32)

        def highest(r, peak):
            fill(r)
            return jnp.maximum(peak, jnp.max(t_ref[...], 0, keepdims=True))

        count = a_ref.shape[0] // tall
        peak = lax.fori_loop(0, count, highest, jnp.full((1, wide), -1e30, F32))

        def add(r, total):
            fill(r)
            return total + jnp.sum(jnp.exp2(t_ref[...] - peak), 0, keepdims=True)

        l_ref[:, cols] = peak + jnp.log2(lax.fori_loop(0, count, add, jnp.zeros((1, wide), F32)))
        return 0

    lax.fori_loop(0, b_ref.shape[1] // wide, column, 0)


def log_sums(a_ref, b_ref, t_refs, l_ref):
    def use(t_ref, rows, cols):
        part = jnp.sum(jnp.exp2(t_ref[...]), 0, keepdims=True)
        l_ref[:, cols] = part if rows.start == 0 else l_ref[:, cols] + part

    blocks(a_ref, b_ref, t_refs, 0, use)
    least = jnp.min(l_ref[...])
    l_ref[...] = jnp.log2(l_ref[...])

    @pl.when(least < LEAST)
    def _():
        exact_logs(a_ref, b_ref, t_refs[0], l_ref)


def by_coordinates(v, p):
    hi, lo = halves(p)
    return jnp.dot(v, hi, preferred_element_type=F32) + jnp.dot(v, lo, preferred_element_type=F32)


def weighted(a_ref, b_ref, v_ref, t_refs, o_ref):
    def use(t_ref, rows, cols):
        part = by_coordinates(v_ref[:, rows], jnp.exp2(t_ref[...]))
        o_ref[:, cols] = part if rows.start == 0 else o_ref[:, cols] + part

    blocks(a_ref, b_ref, t_refs, 0, use)


def row_logs(me_ref, x_hbm, y_hbm, g_hbm, out_ref, x_ref, y_ref, g_ref, a_ref, b_ref, l_ref, t0_ref, t1_ref, sems):
    t_refs = (t0_ref, t1_ref)
    sides = ((y_hbm, y_ref), (x_hbm, x_ref), (g_hbm, g_ref))
    copies = [pltpu.make_async_copy(*pair, sems.at[i]) for i, pair in enumerate(sides)]
    for copy in copies:
        copy.start()
    for copy in copies:
        copy.wait()
    x, y = x_ref[...], y_ref[...]
    y_sq = jnp.sum(y * y, 0, keepdims=True)
    lift = (g_ref[...] - y_sq) * C2
    longest = jnp.sqrt(jnp.sum(x * x, 0, keepdims=True)) * jnp.sqrt(jnp.max(y_sq, 1, keepdims=True))
    bound = jnp.max(lift, 1, keepdims=True) + 2 * C2 * longest
    a_ref[...] = first_side(y, lift).T
    b_ref[...] = second_side(x * (2 * C2), -bound)
    log_sums(a_ref, b_ref, t_refs, l_ref)
    total = l_ref[...] + bound
    for k in range(out_ref.shape[1]):
        for d in range(out_ref.shape[0]):
            out_ref[d, k : k + 1, :] = cut(total, k)


def core_of(me_ref):
    return me_ref[0] >> 3 & 1


def column_sums(log_n, first, me_ref, x_ref, y_ref, g_ref, from_ref, *refs):
    if first:
        pot_ref, total_ref, out_ref, a_ref, v_ref, b_ref, o_ref, l_ref, *t_refs = refs
        parts = from_ref[...]
        top = jnp.max(parts, 0)
        total = top + jnp.log2(jnp.sum(jnp.exp2(parts - top[None]), 0))
        total = jnp.concatenate([total[k : k + 1, :] for k in range(total.shape[0])], 1) + log_n
        total_ref[...] = total
        x = x_ref[...]
        pot_ref[...] = jnp.sum(x * x, 0, keepdims=True) - LN * total
        a_ref[...] = first_side(x * (2 * C2), -total).T
        v_ref[...] = coordinates(x)
    else:
        a_ref, v_ref, out_ref, b_ref, o_ref, l_ref, *t_refs = refs
    half = o_ref.shape[1]
    side = 1 - core_of(me_ref) if first else core_of(me_ref)
    cols = pl.ds(pl.multiple_of(side * half, half), half)
    y = y_ref[:, cols]
    bound = (jnp.sum(y * y, 0, keepdims=True) - g_ref[:, cols]) * C2 - log_n
    b_ref[...] = second_side(y, -bound)
    weighted(a_ref, b_ref, v_ref, t_refs, o_ref)
    mass = o_ref[2 * K : 2 * K + 1, :]
    l_ref[...] = jnp.log2(mass) + bound

    @pl.when(jnp.min(mass) < LEAST)
    def _():
        t_ref = t_refs[0]
        tall, wide = t_ref.shape
        exact_logs(a_ref, b_ref, t_ref, l_ref)
        l_ref[...] += bound
        b_ref[6 * K : KD, :] = offsets(-l_ref[...], False)

        def column(c, _):
            at = pl.ds(pl.multiple_of(c * wide, wide), wide)
            for r in range(0, a_ref.shape[0], tall):
                t_ref[...] = jnp.dot(a_ref[r : r + tall, :], b_ref[:, at], preferred_element_type=F32)
                part = by_coordinates(v_ref[:, r : r + tall], jnp.exp2(t_ref[...]))
                o_ref[:, at] = part if r == 0 else o_ref[:, at] + part
            return 0

        lax.fori_loop(0, half // wide, column, 0)

    for q in range(out_ref.shape[0]):
        at = slice(q * LANES, (q + 1) * LANES)
        out_ref[q, 0:K, :] = (o_ref[0:K, at] + o_ref[K : 2 * K, at]) / o_ref[2 * K : 2 * K + 1, at]
        out_ref[q, K : K + 8, :] = jnp.broadcast_to(l_ref[:, at], (8, LANES))


def merge(logs, images):
    top = functools.reduce(jnp.maximum, logs)
    shares = [jnp.exp2(one - top) for one in logs]
    mass = functools.reduce(jnp.add, shares)
    image = functools.reduce(jnp.add, [w * i for w, i in zip(shares, images)])
    return top + jnp.log2(mass), image / mass


def merge_pair(one_ref, two_ref, out_ref):
    pair, n = (one_ref, two_ref), out_ref.shape[0]
    log, image = merge([ref[:, K : K + 8, :][:, 0:1, :] for ref in pair], [ref[:, 0:K, :] for ref in pair])
    out_ref[:, 0:K, :] = image
    for q in range(n):
        out_ref[0, K + q : K + q + 1, :] = log[q]
    for d in range(1, n):
        out_ref[d, K:, :] = out_ref[0, K:, :]


def merge_logs(part_ref, out_ref):
    parts = [part_ref[d, K:, :] for d in range(part_ref.shape[0])]
    top = functools.reduce(jnp.maximum, parts)
    out_ref[...] = top + jnp.log2(functools.reduce(jnp.add, [jnp.exp2(part - top) for part in parts]))


def merge_chunk(me_ref, part_ref, after_ref, out_ref):
    n = part_ref.shape[0]
    logs = [part_ref[d, pl.ds(K + (me_ref[0] >> 4), 1), :] for d in range(n)]
    _, image = merge(logs, [part_ref[d, 0:K, :] for d in range(n)])
    for d in range(n):
        out_ref[d] = image


def row_images(log_n, me_ref, x_ref, total_ref, after_ref, y_ref, mine_ref, other_ref, pot_ref, out_ref, a_ref, b_ref, v_ref, o_ref, l_ref, *t_refs):
    for part, ref in ((core_of(me_ref), mine_ref), (1 - core_of(me_ref), other_ref)):
        for q in range(ref.shape[0]):
            at = pl.ds(pl.multiple_of((part * ref.shape[0] + q) * LANES, LANES), LANES)
            l_ref[:, at] = ref[q : q + 1, :]
    logs = l_ref[...]
    y = y_ref[...]
    pot_ref[...] = jnp.sum(y * y, 0, keepdims=True) - LN * (logs + log_n)
    a_ref[...] = first_side(y, -logs).T
    b_ref[...] = second_side(x_ref[...] * (2 * C2), LIFT - total_ref[...])
    v_ref[...] = coordinates(y)
    weighted(a_ref, b_ref, v_ref, t_refs, o_ref)
    tiles = o_ref.shape[1] // LANES
    for k in range(tiles):
        lanes = slice(k * LANES, (k + 1) * LANES)
        for r in range(0, K, 8):
            out_ref[r * tiles + 8 * k : r * tiles + 8 * k + 8, :] = o_ref[r : r + 8, lanes] + o_ref[K + r : K + r + 8, lanes]
        out_ref[K * tiles + k : K * tiles + k + 1, :] = o_ref[2 * K : 2 * K + 1, lanes]


def add(one_ref, two_ref, out_ref):
    out_ref[...] = one_ref[...] + two_ref[...]


def add_divide(one_ref, two_ref, out_ref):
    tiles = out_ref.shape[1] // LANES
    mass = one_ref[K * tiles :, :] + two_ref[K * tiles :, :]
    for k in range(tiles):
        under = jnp.broadcast_to(mass[k : k + 1, :], (8, LANES))
        for r in range(0, K, 8):
            at = slice(r * tiles + 8 * k, r * tiles + 8 * k + 8)
            out_ref[r : r + 8, k * LANES : (k + 1) * LANES] = (one_ref[at, :] + two_ref[at, :]) / under


def hold(image_ref, after_ref, out_ref):
    pass


def lay_columns(me_ref, mine_ref, other_ref, out_ref):
    half = out_ref.shape[1] // 2
    for side, ref in ((core_of(me_ref), mine_ref), (1 - core_of(me_ref), other_ref)):
        for q in range(ref.shape[0]):
            out_ref[:, pl.ds(pl.multiple_of(side * half + q * LANES, LANES), LANES)] = ref[q]


def call(kernel, ins, outs, scratch=(), copies=0, aliases={}, cost=None, out="v"):
    spaces = {"s": SM, "h": pl.BlockSpec(memory_space=pltpu.HBM), "v": VM}
    return pl.pallas_call(
        kernel,
        out_shape=tuple(jax.ShapeDtypeStruct(*(one if isinstance(one[0], tuple) else (one, F32))) for one in outs),
        in_specs=[spaces[spec] for spec in ins],
        out_specs=tuple(spaces[out] for _ in outs),
        scratch_shapes=[pltpu.VMEM(*one) for one in scratch] + [pltpu.SemaphoreType.DMA((copies,))] * (copies > 0),
        input_output_aliases=aliases,
        cost_estimate=cost,
        compiler_params=pltpu.CompilerParams(vmem_limit_bytes=50 << 20),
    )


def work(pairs, sums):
    return pl.CostEstimate(flops=2 * pairs * (KD + 256 * sums), transcendentals=pairs, bytes_accessed=8 * pairs)


def solution(mesh):
    n_src, n_tgt = mesh.shape["src"], mesh.shape["tgt"]
    pairs, ring = n_src // 2, n_tgt // 2
    grid = Mesh(mesh.devices.reshape(2, pairs // 2, 2, 2, ring), ("high", "line", "core", "low", "ring"))
    chips, tgt = ("high", "line"), ("low", "ring")
    src = (*chips, "core")
    swap = [(0, 1), (1, 0)]
    over = [(i, (i + ring) % n_tgt) for i in range(n_tgt)]
    near = [(i, i ^ 1) for i in range(n_tgt)]
    far = [(i, i ^ 3) for i in range(n_tgt)]

    def shards(x, y, g):
        ns, nt = x.shape[1], y.shape[1]
        rows = ns // LANES
        me = lax.axis_index(src + tgt).astype(jnp.int32).reshape(1)
        g = g.reshape(1, nt)
        chunk = (pairs, K + 8, LANES)

        part, x, y, g = call(
            row_logs,
            "shhh",
            [(n_tgt, rows, LANES), x.shape, y.shape, g.shape],
            [((nt, KD), BF), ((KD, ns), BF), ((1, ns), F32), BLOCK, BLOCK],
            3,
            cost=work(ns * nt, 0),
        )(me, *(pltpu.with_memory_space_constraint(one, pltpu.HBM) for one in (x, y, g)))
        part = lax.all_to_all(part, tgt, 0, 0, tiled=True)

        sums = [((KD, nt // 2), BF), ((80, nt // 2), F32), ((1, nt // 2), F32), BLOCK, BLOCK]
        log_n = math.log2(ns * n_src)
        source_potential, total, send, side, weights = call(
            functools.partial(column_sums, log_n, True),
            "svvvv",
            [(1, ns), (1, ns), chunk, ((ns, KD), BF), ((80, ns), BF)],
            sums,
            cost=work(ns * nt // 2, 2),
        )(me, x, y, g, part)
        sent = lax.ppermute(send, "core", swap)
        (keep,) = call(
            functools.partial(column_sums, log_n, False), "svvvvvv", [chunk], sums, cost=work(ns * nt // 2, 2)
        )(me, x, y, g, total, side, weights)
        (part,) = call(merge_pair, "vv", [(pairs, K + pairs, LANES)])(keep, sent)
        image = lax.all_to_all(part, chips, 0, 0, tiled=True)
        (mine,) = call(merge_logs, "v", [(pairs, LANES)])(image)
        other = lax.ppermute(mine, "core", swap)

        (image,) = call(merge_chunk, "svv", [(pairs, K, LANES)], cost=work(ns * nt // 2, 2))(me, image, mine)

        tall = (K * ns) // LANES
        target_potential, held = call(
            functools.partial(row_images, math.log2(nt * n_tgt)),
            "svvhvvv",
            [(1, nt), (tall + rows, LANES)],
            [((nt, KD), BF), ((KD, ns), BF), ((80, nt), BF), ((80, ns), F32), ((1, nt), F32), BLOCK, BLOCK],
            cost=work(ns * nt, 2),
        )(me, x, total, image, y, mine, other)
        (image,) = call(hold, "hv", [image.shape], aliases={0: 0}, out="h")(image, held)
        image = lax.all_to_all(image, chips, 0, 0, tiled=True)
        sizes = [held.shape]
        (held,) = call(add, "vv", sizes, cost=work(ns * nt // 4, 2))(held, lax.ppermute(held, tgt, over))
        (held,) = call(add, "vv", sizes, cost=work(ns * nt // 4, 2))(held, lax.ppermute(held, tgt, near))
        (source_image,) = call(add_divide, "vv", [(K, ns)], cost=work(ns * nt // 4, 2))(
            held, lax.ppermute(held, tgt, far)
        )
        (image,) = call(hold, "vv", [image.shape], aliases={0: 0})(image, held)
        (target_image,) = call(lay_columns, "svv", [(K, nt)])(me, image, lax.ppermute(image, "core", swap))
        return source_potential.reshape(ns), target_potential.reshape(nt), source_image, target_image

    return jax.shard_map(
        shards,
        mesh=grid,
        in_specs=(P(None, src), P(None, tgt), P(tgt)),
        out_specs=(P(src), P(tgt), P(None, src), P(None, tgt)),
        check_vma=False,
    )
```

```python
import functools
import math

import jax
import jax.numpy as jnp
from jax import lax
from jax.experimental import pallas as pl
from jax.experimental.pallas import tpu as pltpu
from jax.sharding import Mesh
from jax.sharding import PartitionSpec as P

EPS = 0.05
C2 = 1.4426950408889634 / EPS
LN = EPS * math.log(2.0)
LEAST = 2.0**-80
LIFT = 64.0
BF = jnp.bfloat16
F32 = jnp.float32
K = 32
KD = 8 * K
VM = pl.BlockSpec(memory_space=pltpu.VMEM)
SM = pl.BlockSpec(memory_space=pltpu.SMEM)
LANES = 128
TALL, WIDE = 1024, 256
BLOCK = ((TALL, WIDE), F32)


def thirds(v):
    hi = v.astype(BF)
    rest = v - hi.astype(F32)
    mid = rest.astype(BF)
    return hi, mid, (rest - mid.astype(F32)).astype(BF)


def halves(v):
    hi = v.astype(BF)
    return hi, (v - hi.astype(F32)).astype(BF)


def offsets(b, first):
    hi, mid, lo = (part.astype(F32) for part in thirds(b))
    row = lax.broadcasted_iota(jnp.int32, (2 * K, b.shape[1]), 0)
    row, one = (row, row - 3) if first else (row - 3, row)
    value = jnp.where(row == 0, hi, jnp.where(row == 1, mid, jnp.where(row == 2, lo, 0.0)))
    return jnp.where((one >= 0) & (one < 3), 1.0, value).astype(BF)


def first_side(v, b):
    hi, mid, lo = thirds(v)
    return jnp.concatenate([hi, hi, hi, mid, mid, lo, offsets(b, True)], 0)


def second_side(v, b):
    hi, mid, lo = thirds(v)
    return jnp.concatenate([hi, mid, lo, hi, mid, hi, offsets(b, False)], 0)


def coordinates(v):
    hi, lo = halves(v)
    return jnp.concatenate([hi, lo, jnp.ones((K // 2, v.shape[1]), BF)], 0)


def cut(tiles, k):
    return tiles[:, k * LANES : (k + 1) * LANES]


def blocks(a_ref, b_ref, t_refs, first, use):
    tall, wide = t_refs[0].shape
    places = [(r, c) for c in range(first, first + b_ref.shape[1], wide) for r in range(0, a_ref.shape[0], tall)]

    def fill(i):
        r, c = places[i]
        t_refs[i % 2][...] = jnp.dot(a_ref[r : r + tall, :], b_ref[:, c : c + wide], preferred_element_type=F32)

    fill(0)
    for i, (r, c) in enumerate(places):
        if i + 1 < len(places):
            fill(i + 1)
        use(t_refs[i % 2], slice(r, r + tall), slice(c, c + wide))


def exact_logs(a_ref, b_ref, t_ref, l_ref):
    tall, wide = t_ref.shape

    def column(c, _):
        cols = pl.ds(pl.multiple_of(c * wide, wide), wide)

        def fill(r):
            rows = pl.ds(pl.multiple_of(r * tall, tall), tall)
            t_ref[...] = jnp.dot(a_ref[rows, :], b_ref[:, cols], preferred_element_type=F32)

        def highest(r, peak):
            fill(r)
            return jnp.maximum(peak, jnp.max(t_ref[...], 0, keepdims=True))

        count = a_ref.shape[0] // tall
        peak = lax.fori_loop(0, count, highest, jnp.full((1, wide), -1e30, F32))

        def add(r, total):
            fill(r)
            return total + jnp.sum(jnp.exp2(t_ref[...] - peak), 0, keepdims=True)

        l_ref[:, cols] = peak + jnp.log2(lax.fori_loop(0, count, add, jnp.zeros((1, wide), F32)))
        return 0

    lax.fori_loop(0, b_ref.shape[1] // wide, column, 0)


def plain_sums(a_ref, b_ref, t_refs, l_ref):
    def use(t_ref, rows, cols):
        part = jnp.sum(jnp.exp2(t_ref[...]), 0, keepdims=True)
        l_ref[:, cols] = part if rows.start == 0 else l_ref[:, cols] + part

    blocks(a_ref, b_ref, t_refs, 0, use)


def by_coordinates(v, p):
    hi, lo = halves(p)
    return jnp.dot(v, hi, preferred_element_type=F32) + jnp.dot(v, lo, preferred_element_type=F32)


def weighted(a_ref, b_ref, v_ref, t_refs, o_ref):
    def use(t_ref, rows, cols):
        part = by_coordinates(v_ref[:, rows], jnp.exp2(t_ref[...]))
        o_ref[:, cols] = part if rows.start == 0 else o_ref[:, cols] + part

    blocks(a_ref, b_ref, t_refs, 0, use)


def row_logs(me_ref, x_hbm, y_hbm, g_hbm, out_ref, x_ref, y_ref, g_ref, a_ref, b_ref, l_ref, t0_ref, t1_ref, sems):
    t_refs = (t0_ref, t1_ref)
    sides = ((y_hbm, y_ref), (x_hbm, x_ref), (g_hbm, g_ref))
    copies = [pltpu.make_async_copy(*pair, sems.at[i]) for i, pair in enumerate(sides)]
    for copy in copies:
        copy.start()
    for copy in copies:
        copy.wait()
    x, y = x_ref[...], y_ref[...]
    y_sq = jnp.sum(y * y, 0, keepdims=True)
    lift = (g_ref[...] - y_sq) * C2
    longest = jnp.sqrt(jnp.sum(x * x, 0, keepdims=True)) * jnp.sqrt(jnp.max(y_sq, 1, keepdims=True))
    bound = jnp.max(lift, 1, keepdims=True) + 2 * C2 * longest
    a_ref[...] = first_side(y, lift).T
    b_ref[...] = second_side(x * (2 * C2), -bound)
    plain_sums(a_ref, b_ref, t_refs, l_ref)
    sums = l_ref[...]

    def finish(logs):
        total = logs + bound
        tile = jnp.concatenate([cut(total, k) for k in range(out_ref.shape[1])], 0)
        for d in range(out_ref.shape[0]):
            out_ref[d] = tile

    finish(jnp.log2(sums))

    @pl.when(jnp.min(sums) < LEAST)
    def _():
        exact_logs(a_ref, b_ref, t_refs[0], l_ref)
        finish(l_ref[...])


def core_of(me_ref):
    return me_ref[0] >> 3 & 1


def column_sums(log_n, first, me_ref, x_ref, y_ref, g_ref, from_ref, *refs):
    if first:
        pot_ref, total_ref, out_ref, a_ref, v_ref, b_ref, o_ref, l_ref, *t_refs = refs
        parts = from_ref[...]
        top = jnp.max(parts, 0)
        total = top + jnp.log2(jnp.sum(jnp.exp2(parts - top[None]), 0))
        total = jnp.concatenate([total[k : k + 1, :] for k in range(total.shape[0])], 1) + log_n
        total_ref[...] = total
        x = x_ref[...]
        pot_ref[...] = jnp.sum(x * x, 0, keepdims=True) - LN * total
        a_ref[...] = first_side(x * (2 * C2), -total).T
        v_ref[...] = coordinates(x)
    else:
        a_ref, v_ref, out_ref, b_ref, o_ref, l_ref, *t_refs = refs
    half = o_ref.shape[1]
    side = 1 - core_of(me_ref) if first else core_of(me_ref)
    cols = pl.ds(pl.multiple_of(side * half, half), half)
    y = y_ref[:, cols]
    bound = (jnp.sum(y * y, 0, keepdims=True) - g_ref[:, cols]) * C2 - log_n
    b_ref[...] = second_side(y, -bound)
    weighted(a_ref, b_ref, v_ref, t_refs, o_ref)
    mass = o_ref[2 * K : 2 * K + 1, :]

    def finish(logs):
        share = 1.0 / o_ref[2 * K : 2 * K + 1, :]
        for q in range(out_ref.shape[0]):
            at = slice(q * LANES, (q + 1) * LANES)
            out_ref[q, 0:K, :] = (o_ref[0:K, at] + o_ref[K : 2 * K, at]) * share[:, at]
            out_ref[q, K : K + 8, :] = jnp.broadcast_to(logs[:, at], (8, LANES))

    finish(jnp.log2(mass) + bound)

    @pl.when(jnp.min(mass) < LEAST)
    def _():
        t_ref = t_refs[0]
        tall, wide = t_ref.shape
        exact_logs(a_ref, b_ref, t_ref, l_ref)
        l_ref[...] += bound
        b_ref[6 * K : KD, :] = offsets(-l_ref[...], False)

        def column(c, _):
            at = pl.ds(pl.multiple_of(c * wide, wide), wide)
            for r in range(0, a_ref.shape[0], tall):
                t_ref[...] = jnp.dot(a_ref[r : r + tall, :], b_ref[:, at], preferred_element_type=F32)
                part = by_coordinates(v_ref[:, r : r + tall], jnp.exp2(t_ref[...]))
                o_ref[:, at] = part if r == 0 else o_ref[:, at] + part
            return 0

        lax.fori_loop(0, half // wide, column, 0)
        finish(l_ref[...])


def merge(logs, images):
    top = functools.reduce(jnp.maximum, logs)
    shares = [jnp.exp2(one - top) for one in logs]
    mass = functools.reduce(jnp.add, shares)
    image = functools.reduce(jnp.add, [w * i for w, i in zip(shares, images)])
    return top + jnp.log2(mass), image / mass


def merge_pair(one_ref, two_ref, out_ref):
    pair, n = (one_ref, two_ref), out_ref.shape[0]
    log, image = merge([ref[:, K : K + 8, :][:, 0:1, :] for ref in pair], [ref[:, 0:K, :] for ref in pair])
    out_ref[:, 0:K, :] = image
    for q in range(n):
        out_ref[0, K + q : K + q + 1, :] = log[q]
    for d in range(1, n):
        out_ref[d, K:, :] = out_ref[0, K:, :]


def merge_logs(part_ref, out_ref):
    parts = [part_ref[d, K:, :] for d in range(part_ref.shape[0])]
    top = functools.reduce(jnp.maximum, parts)
    out_ref[...] = top + jnp.log2(functools.reduce(jnp.add, [jnp.exp2(part - top) for part in parts]))


def merge_chunk(me_ref, part_ref, after_ref, out_ref):
    n = part_ref.shape[0]
    logs = [part_ref[d, pl.ds(K + (me_ref[0] >> 4), 1), :] for d in range(n)]
    _, image = merge(logs, [part_ref[d, 0:K, :] for d in range(n)])
    for d in range(n):
        out_ref[d] = image


def row_images(log_n, me_ref, x_ref, total_ref, after_ref, y_ref, mine_ref, other_ref, pot_ref, out_ref, a_ref, b_ref, v_ref, o_ref, l_ref, *t_refs):
    for part, ref in ((core_of(me_ref), mine_ref), (1 - core_of(me_ref), other_ref)):
        for q in range(ref.shape[0]):
            at = pl.ds(pl.multiple_of((part * ref.shape[0] + q) * LANES, LANES), LANES)
            l_ref[:, at] = ref[q : q + 1, :]
    logs = l_ref[...]
    y = y_ref[...]
    pot_ref[...] = jnp.sum(y * y, 0, keepdims=True) - LN * (logs + log_n)
    a_ref[...] = first_side(y, -logs).T
    b_ref[...] = second_side(x_ref[...] * (2 * C2), LIFT - total_ref[...])
    v_ref[...] = coordinates(y)
    weighted(a_ref, b_ref, v_ref, t_refs, o_ref)
    tiles = o_ref.shape[1] // LANES
    for k in range(tiles):
        lanes = slice(k * LANES, (k + 1) * LANES)
        for r in range(0, K, 8):
            out_ref[r * tiles + 8 * k : r * tiles + 8 * k + 8, :] = o_ref[r : r + 8, lanes] + o_ref[K + r : K + r + 8, lanes]
        out_ref[K * tiles + k : K * tiles + k + 1, :] = o_ref[2 * K : 2 * K + 1, lanes]


def add(one_ref, two_ref, out_ref):
    out_ref[...] = one_ref[...] + two_ref[...]


def add_divide(one_ref, two_ref, out_ref):
    tiles = out_ref.shape[1] // LANES
    mass = one_ref[K * tiles :, :] + two_ref[K * tiles :, :]
    for k in range(tiles):
        under = jnp.broadcast_to(mass[k : k + 1, :], (8, LANES))
        for r in range(0, K, 8):
            at = slice(r * tiles + 8 * k, r * tiles + 8 * k + 8)
            out_ref[r : r + 8, k * LANES : (k + 1) * LANES] = (one_ref[at, :] + two_ref[at, :]) / under


def hold(image_ref, after_ref, out_ref):
    pass


def lay_columns(me_ref, mine_ref, other_ref, out_ref):
    half = out_ref.shape[1] // 2
    for side, ref in ((core_of(me_ref), mine_ref), (1 - core_of(me_ref), other_ref)):
        for q in range(ref.shape[0]):
            out_ref[:, pl.ds(pl.multiple_of(side * half + q * LANES, LANES), LANES)] = ref[q]


def call(kernel, ins, outs, scratch=(), copies=0, aliases={}, cost=None, out="v"):
    spaces = {"s": SM, "h": pl.BlockSpec(memory_space=pltpu.HBM), "v": VM}
    return pl.pallas_call(
        kernel,
        out_shape=tuple(jax.ShapeDtypeStruct(*(one if isinstance(one[0], tuple) else (one, F32))) for one in outs),
        in_specs=[spaces[spec] for spec in ins],
        out_specs=tuple(spaces[out] for _ in outs),
        scratch_shapes=[pltpu.VMEM(*one) for one in scratch] + [pltpu.SemaphoreType.DMA((copies,))] * (copies > 0),
        input_output_aliases=aliases,
        cost_estimate=cost,
        compiler_params=pltpu.CompilerParams(vmem_limit_bytes=50 << 20),
    )


def work(pairs, sums):
    return pl.CostEstimate(flops=2 * pairs * (KD + 256 * sums), transcendentals=pairs, bytes_accessed=8 * pairs)


def solution(mesh):
    n_src, n_tgt = mesh.shape["src"], mesh.shape["tgt"]
    pairs, ring = n_src // 2, n_tgt // 2
    grid = Mesh(mesh.devices.reshape(2, pairs // 2, 2, 2, ring), ("high", "line", "core", "low", "ring"))
    chips, tgt = ("high", "line"), ("low", "ring")
    src = (*chips, "core")
    swap = [(0, 1), (1, 0)]
    over = [(i, (i + ring) % n_tgt) for i in range(n_tgt)]
    near = [(i, i ^ 1) for i in range(n_tgt)]
    far = [(i, i ^ 3) for i in range(n_tgt)]

    def shards(x, y, g):
        ns, nt = x.shape[1], y.shape[1]
        rows = ns // LANES
        me = lax.axis_index(src + tgt).astype(jnp.int32).reshape(1)
        g = g.reshape(1, nt)
        chunk = (pairs, K + 8, LANES)

        part, x, y, g = call(
            row_logs,
            "shhh",
            [(n_tgt, rows, LANES), x.shape, y.shape, g.shape],
            [((nt, KD), BF), ((KD, ns), BF), ((1, ns), F32), BLOCK, BLOCK],
            3,
            cost=work(ns * nt, 0),
        )(me, *(pltpu.with_memory_space_constraint(one, pltpu.HBM) for one in (x, y, g)))
        part = lax.all_to_all(part, tgt, 0, 0, tiled=True)

        sums = [((KD, nt // 2), BF), ((80, nt // 2), F32), ((1, nt // 2), F32), BLOCK, BLOCK]
        log_n = math.log2(ns * n_src)
        source_potential, total, send, side, weights = call(
            functools.partial(column_sums, log_n, True),
            "svvvv",
            [(1, ns), (1, ns), chunk, ((ns, KD), BF), ((80, ns), BF)],
            sums,
            cost=work(ns * nt // 2, 2),
        )(me, x, y, g, part)
        sent = lax.ppermute(send, "core", swap)
        (keep,) = call(
            functools.partial(column_sums, log_n, False), "svvvvvv", [chunk], sums, cost=work(ns * nt // 2, 2)
        )(me, x, y, g, total, side, weights)
        (part,) = call(merge_pair, "vv", [(pairs, K + pairs, LANES)])(keep, sent)
        image = lax.all_to_all(part, chips, 0, 0, tiled=True)
        (mine,) = call(merge_logs, "v", [(pairs, LANES)])(image)
        other = lax.ppermute(mine, "core", swap)

        (image,) = call(merge_chunk, "svv", [(pairs, K, LANES)], cost=work(ns * nt // 2, 2))(me, image, mine)

        tall = (K * ns) // LANES
        target_potential, held = call(
            functools.partial(row_images, math.log2(nt * n_tgt)),
            "svvhvvv",
            [(1, nt), (tall + rows, LANES)],
            [((nt, KD), BF), ((KD, ns), BF), ((80, nt), BF), ((80, ns), F32), ((1, nt), F32), BLOCK, BLOCK],
            cost=work(ns * nt, 2),
        )(me, x, total, image, y, mine, other)
        (image,) = call(hold, "hv", [image.shape], aliases={0: 0}, out="h")(image, held)
        image = lax.all_to_all(image, chips, 0, 0, tiled=True)
        sizes = [held.shape]
        (held,) = call(add, "vv", sizes, cost=work(ns * nt // 4, 2))(held, lax.ppermute(held, tgt, near))
        (held,) = call(add, "vv", sizes, cost=work(ns * nt // 4, 2))(held, lax.ppermute(held, tgt, far))
        (source_image,) = call(add_divide, "vv", [(K, ns)], cost=work(ns * nt // 4, 2))(
            held, lax.ppermute(held, tgt, over)
        )
        (image,) = call(hold, "vv", [image.shape], aliases={0: 0})(image, held)
        (target_image,) = call(lay_columns, "svv", [(K, nt)])(me, image, lax.ppermute(image, "core", swap))
        return source_potential.reshape(ns), target_potential.reshape(nt), source_image, target_image

    return jax.shard_map(
        shards,
        mesh=grid,
        in_specs=(P(None, src), P(None, tgt), P(tgt)),
        out_specs=(P(src), P(tgt), P(None, src), P(None, tgt)),
        check_vma=False,
    )
```

```python
import functools
import math

import jax
import jax.numpy as jnp
from jax import lax
from jax.experimental import pallas as pl
from jax.experimental.pallas import tpu as pltpu
from jax.sharding import Mesh
from jax.sharding import PartitionSpec as P

EPS = 0.05
C2 = 1.4426950408889634 / EPS
LN = EPS * math.log(2.0)
LEAST = 2.0**-80
LIFT = 64.0
BF = jnp.bfloat16
F32 = jnp.float32
K = 32
KD = 8 * K
VM = pl.BlockSpec(memory_space=pltpu.VMEM)
SM = pl.BlockSpec(memory_space=pltpu.SMEM)
LANES = 128
TALL, WIDE = 1024, 256
BLOCK = ((TALL, WIDE), F32)


def thirds(v):
    hi = v.astype(BF)
    rest = v - hi.astype(F32)
    mid = rest.astype(BF)
    return hi, mid, (rest - mid.astype(F32)).astype(BF)


def halves(v):
    hi = v.astype(BF)
    return hi, (v - hi.astype(F32)).astype(BF)


def offsets(b, first):
    hi, mid, lo = (part.astype(F32) for part in thirds(b))
    row = lax.broadcasted_iota(jnp.int32, (2 * K, b.shape[1]), 0)
    row, one = (row, row - 3) if first else (row - 3, row)
    value = jnp.where(row == 0, hi, jnp.where(row == 1, mid, jnp.where(row == 2, lo, 0.0)))
    return jnp.where((one >= 0) & (one < 3), 1.0, value).astype(BF)


def first_side(v, b):
    hi, mid, lo = thirds(v)
    return jnp.concatenate([hi, hi, hi, mid, mid, lo, offsets(b, True)], 0)


def second_side(v, b):
    hi, mid, lo = thirds(v)
    return jnp.concatenate([hi, mid, lo, hi, mid, hi, offsets(b, False)], 0)


def coordinates(v):
    hi, lo = halves(v)
    return jnp.concatenate([hi, lo, jnp.ones((K // 2, v.shape[1]), BF)], 0)


def cut(tiles, k):
    return tiles[:, k * LANES : (k + 1) * LANES]


def blocks(a_ref, b_ref, t_refs, first, use):
    tall, wide = t_refs[0].shape
    places = [(r, c) for c in range(first, first + b_ref.shape[1], wide) for r in range(0, a_ref.shape[0], tall)]

    def fill(i):
        r, c = places[i]
        t_refs[i % 2][...] = jnp.dot(a_ref[r : r + tall, :], b_ref[:, c : c + wide], preferred_element_type=F32)

    fill(0)
    for i, (r, c) in enumerate(places):
        if i + 1 < len(places):
            fill(i + 1)
        use(t_refs[i % 2], slice(r, r + tall), slice(c, c + wide))


def exact_logs(a_ref, b_ref, t_ref, l_ref):
    tall, wide = t_ref.shape

    def column(c, _):
        cols = pl.ds(pl.multiple_of(c * wide, wide), wide)

        def fill(r):
            rows = pl.ds(pl.multiple_of(r * tall, tall), tall)
            t_ref[...] = jnp.dot(a_ref[rows, :], b_ref[:, cols], preferred_element_type=F32)

        def highest(r, peak):
            fill(r)
            return jnp.maximum(peak, jnp.max(t_ref[...], 0, keepdims=True))

        count = a_ref.shape[0] // tall
        peak = lax.fori_loop(0, count, highest, jnp.full((1, wide), -1e30, F32))

        def add(r, total):
            fill(r)
            return total + jnp.sum(jnp.exp2(t_ref[...] - peak), 0, keepdims=True)

        l_ref[:, cols] = peak + jnp.log2(lax.fori_loop(0, count, add, jnp.zeros((1, wide), F32)))
        return 0

    lax.fori_loop(0, b_ref.shape[1] // wide, column, 0)


def plain_sums(a_ref, b_ref, t_refs, l_ref):
    def use(t_ref, rows, cols):
        part = jnp.sum(jnp.exp2(t_ref[...]), 0, keepdims=True)
        l_ref[:, cols] = part if rows.start == 0 else l_ref[:, cols] + part

    blocks(a_ref, b_ref, t_refs, 0, use)


def by_coordinates(v, p):
    hi, lo = halves(p)
    return jnp.dot(v, hi, preferred_element_type=F32) + jnp.dot(v, lo, preferred_element_type=F32)


def weighted(a_ref, b_ref, v_ref, t_refs, o_ref):
    def use(t_ref, rows, cols):
        part = by_coordinates(v_ref[:, rows], jnp.exp2(t_ref[...]))
        o_ref[:, cols] = part if rows.start == 0 else o_ref[:, cols] + part

    blocks(a_ref, b_ref, t_refs, 0, use)


def row_logs(me_ref, x_hbm, y_hbm, g_hbm, out_ref, x_ref, y_ref, g_ref, a_ref, b_ref, l_ref, t0_ref, t1_ref, sems):
    t_refs = (t0_ref, t1_ref)
    sides = ((y_hbm, y_ref), (x_hbm, x_ref), (g_hbm, g_ref))
    copies = [pltpu.make_async_copy(*pair, sems.at[i]) for i, pair in enumerate(sides)]
    for copy in copies:
        copy.start()
    for copy in copies:
        copy.wait()
    x, y = x_ref[...], y_ref[...]
    y_sq = jnp.sum(y * y, 0, keepdims=True)
    lift = (g_ref[...] - y_sq) * C2
    longest = jnp.sqrt(jnp.sum(x * x, 0, keepdims=True)) * jnp.sqrt(jnp.max(y_sq, 1, keepdims=True))
    bound = jnp.max(lift, 1, keepdims=True) + 2 * C2 * longest
    a_ref[...] = first_side(y, lift).T
    b_ref[...] = second_side(x * (2 * C2), -bound)
    plain_sums(a_ref, b_ref, t_refs, l_ref)
    sums = l_ref[...]

    def finish(logs):
        total = logs + bound
        tile = jnp.concatenate([cut(total, k) for k in range(out_ref.shape[1])], 0)
        for d in range(out_ref.shape[0]):
            out_ref[d] = tile

    finish(jnp.log2(sums))

    @pl.when(jnp.min(sums) < LEAST)
    def _():
        exact_logs(a_ref, b_ref, t_refs[0], l_ref)
        finish(l_ref[...])


def core_of(me_ref):
    return me_ref[0] >> 3 & 1


def column_sums(log_n, first, me_ref, x_ref, y_ref, g_ref, from_ref, *refs):
    if first:
        pot_ref, total_ref, out_ref, a_ref, v_ref, b_ref, o_ref, l_ref, *t_refs = refs
        parts = from_ref[...]
        top = jnp.max(parts, 0)
        total = top + jnp.log2(jnp.sum(jnp.exp2(parts - top[None]), 0))
        total = jnp.concatenate([total[k : k + 1, :] for k in range(total.shape[0])], 1) + log_n
        total_ref[...] = total
        x = x_ref[...]
        pot_ref[...] = jnp.sum(x * x, 0, keepdims=True) - LN * total
        a_ref[...] = first_side(x * (2 * C2), -total).T
        v_ref[...] = coordinates(x)
    else:
        a_ref, v_ref, out_ref, b_ref, o_ref, l_ref, *t_refs = refs
    half = o_ref.shape[1]
    side = 1 - core_of(me_ref) if first else core_of(me_ref)
    cols = pl.ds(pl.multiple_of(side * half, half), half)
    y = y_ref[:, cols]
    bound = (jnp.sum(y * y, 0, keepdims=True) - g_ref[:, cols]) * C2 - log_n
    b_ref[...] = second_side(y, -bound)
    weighted(a_ref, b_ref, v_ref, t_refs, o_ref)
    mass = o_ref[2 * K : 2 * K + 1, :]

    def finish(logs):
        share = 1.0 / o_ref[2 * K : 2 * K + 1, :]
        for q in range(out_ref.shape[0]):
            at = slice(q * LANES, (q + 1) * LANES)
            out_ref[q, 0:K, :] = (o_ref[0:K, at] + o_ref[K : 2 * K, at]) * share[:, at]
            out_ref[q, K : K + 8, :] = jnp.broadcast_to(logs[:, at], (8, LANES))

    finish(jnp.log2(mass) + bound)

    @pl.when(jnp.min(mass) < LEAST)
    def _():
        t_ref = t_refs[0]
        tall, wide = t_ref.shape
        exact_logs(a_ref, b_ref, t_ref, l_ref)
        l_ref[...] += bound
        b_ref[6 * K : KD, :] = offsets(-l_ref[...], False)

        def column(c, _):
            at = pl.ds(pl.multiple_of(c * wide, wide), wide)
            for r in range(0, a_ref.shape[0], tall):
                t_ref[...] = jnp.dot(a_ref[r : r + tall, :], b_ref[:, at], preferred_element_type=F32)
                part = by_coordinates(v_ref[:, r : r + tall], jnp.exp2(t_ref[...]))
                o_ref[:, at] = part if r == 0 else o_ref[:, at] + part
            return 0

        lax.fori_loop(0, half // wide, column, 0)
        finish(l_ref[...])


def merge(logs, images):
    top = functools.reduce(jnp.maximum, logs)
    shares = [jnp.exp2(one - top) for one in logs]
    mass = functools.reduce(jnp.add, shares)
    image = functools.reduce(jnp.add, [w * i for w, i in zip(shares, images)])
    return top + jnp.log2(mass), image / mass


def merge_pair(one_ref, two_ref, out_ref):
    pair, n = (one_ref, two_ref), out_ref.shape[0]
    log, image = merge([ref[:, K : K + 8, :][:, 0:1, :] for ref in pair], [ref[:, 0:K, :] for ref in pair])
    out_ref[:, 0:K, :] = image
    for q in range(n):
        out_ref[0, K + q : K + q + 1, :] = log[q]
    for d in range(1, n):
        out_ref[d, K:, :] = out_ref[0, K:, :]


def merge_logs(part_ref, out_ref):
    parts = [part_ref[d, K:, :] for d in range(part_ref.shape[0])]
    top = functools.reduce(jnp.maximum, parts)
    out_ref[...] = top + jnp.log2(functools.reduce(jnp.add, [jnp.exp2(part - top) for part in parts]))


def merge_chunk(me_ref, part_ref, after_ref, out_ref):
    n = part_ref.shape[0]
    logs = [part_ref[d, pl.ds(K + (me_ref[0] >> 4), 1), :] for d in range(n)]
    _, image = merge(logs, [part_ref[d, 0:K, :] for d in range(n)])
    for d in range(n):
        out_ref[d] = image


def row_images(log_n, me_ref, x_ref, total_ref, after_ref, y_ref, mine_ref, other_ref, pot_ref, out_ref, a_ref, b_ref, v_ref, o_ref, l_ref, *t_refs):
    for part, ref in ((core_of(me_ref), mine_ref), (1 - core_of(me_ref), other_ref)):
        for q in range(ref.shape[0]):
            at = pl.ds(pl.multiple_of((part * ref.shape[0] + q) * LANES, LANES), LANES)
            l_ref[:, at] = ref[q : q + 1, :]
    logs = l_ref[...]
    y = y_ref[...]
    pot_ref[...] = jnp.sum(y * y, 0, keepdims=True) - LN * (logs + log_n)
    a_ref[...] = first_side(y, -logs).T
    b_ref[...] = second_side(x_ref[...] * (2 * C2), LIFT - total_ref[...])
    v_ref[...] = coordinates(y)
    weighted(a_ref, b_ref, v_ref, t_refs, o_ref)
    tiles = o_ref.shape[1] // LANES
    for k in range(tiles):
        lanes = slice(k * LANES, (k + 1) * LANES)
        for r in range(0, K, 8):
            out_ref[r * tiles + 8 * k : r * tiles + 8 * k + 8, :] = o_ref[r : r + 8, lanes] + o_ref[K + r : K + r + 8, lanes]
        out_ref[K * tiles + k : K * tiles + k + 1, :] = o_ref[2 * K : 2 * K + 1, lanes]


def add(one_ref, two_ref, out_ref):
    out_ref[...] = one_ref[...] + two_ref[...]


def add_divide(one_ref, two_ref, src_ref, tgt_ref, out_ref, src_out_ref, tgt_out_ref):
    src_out_ref[...] = src_ref[...]
    tgt_out_ref[...] = tgt_ref[...]
    tiles = out_ref.shape[1] // LANES
    mass = one_ref[K * tiles :, :] + two_ref[K * tiles :, :]
    for k in range(tiles):
        under = jnp.broadcast_to(mass[k : k + 1, :], (8, LANES))
        for r in range(0, K, 8):
            at = slice(r * tiles + 8 * k, r * tiles + 8 * k + 8)
            out_ref[r : r + 8, k * LANES : (k + 1) * LANES] = (one_ref[at, :] + two_ref[at, :]) / under


def hold(image_ref, after_ref, out_ref):
    pass


def lay_columns(me_ref, mine_ref, other_ref, out_ref):
    half = out_ref.shape[1] // 2
    for side, ref in ((core_of(me_ref), mine_ref), (1 - core_of(me_ref), other_ref)):
        for q in range(ref.shape[0]):
            out_ref[:, pl.ds(pl.multiple_of(side * half + q * LANES, LANES), LANES)] = ref[q]


def call(kernel, ins, outs, scratch=(), copies=0, aliases={}, cost=None, out="v"):
    spaces = {"s": SM, "h": pl.BlockSpec(memory_space=pltpu.HBM), "v": VM}
    return pl.pallas_call(
        kernel,
        out_shape=tuple(jax.ShapeDtypeStruct(*(one if isinstance(one[0], tuple) else (one, F32))) for one in outs),
        in_specs=[spaces[spec] for spec in ins],
        out_specs=tuple(spaces[out] for _ in outs),
        scratch_shapes=[pltpu.VMEM(*one) for one in scratch] + [pltpu.SemaphoreType.DMA((copies,))] * (copies > 0),
        input_output_aliases=aliases,
        cost_estimate=cost,
        compiler_params=pltpu.CompilerParams(vmem_limit_bytes=50 << 20),
    )


def work(pairs, sums):
    return pl.CostEstimate(flops=2 * pairs * (KD + 256 * sums), transcendentals=pairs, bytes_accessed=8 * pairs)


def solution(mesh):
    n_src, n_tgt = mesh.shape["src"], mesh.shape["tgt"]
    pairs, ring = n_src // 2, n_tgt // 2
    grid = Mesh(mesh.devices.reshape(2, pairs // 2, 2, 2, ring), ("high", "line", "core", "low", "ring"))
    chips, tgt = ("high", "line"), ("low", "ring")
    src = (*chips, "core")
    swap = [(0, 1), (1, 0)]
    over = [(i, (i + ring) % n_tgt) for i in range(n_tgt)]
    near = [(i, i ^ 1) for i in range(n_tgt)]
    far = [(i, i ^ 3) for i in range(n_tgt)]

    def shards(x, y, g):
        ns, nt = x.shape[1], y.shape[1]
        rows = ns // LANES
        me = lax.axis_index(src + tgt).astype(jnp.int32).reshape(1)
        g = g.reshape(1, nt)
        chunk = (pairs, K + 8, LANES)

        part, x, y, g = call(
            row_logs,
            "shhh",
            [(n_tgt, rows, LANES), x.shape, y.shape, g.shape],
            [((nt, KD), BF), ((KD, ns), BF), ((1, ns), F32), BLOCK, BLOCK],
            3,
            cost=work(ns * nt, 0),
        )(me, *(pltpu.with_memory_space_constraint(one, pltpu.HBM) for one in (x, y, g)))
        part = lax.all_to_all(part, tgt, 0, 0, tiled=True)

        sums = [((KD, nt // 2), BF), ((80, nt // 2), F32), ((1, nt // 2), F32), BLOCK, BLOCK]
        log_n = math.log2(ns * n_src)
        source_potential, total, send, side, weights = call(
            functools.partial(column_sums, log_n, True),
            "svvvv",
            [(1, ns), (1, ns), chunk, ((ns, KD), BF), ((80, ns), BF)],
            sums,
            cost=work(ns * nt // 2, 2),
        )(me, x, y, g, part)
        sent = lax.ppermute(send, "core", swap)
        (keep,) = call(
            functools.partial(column_sums, log_n, False), "svvvvvv", [chunk], sums, cost=work(ns * nt // 2, 2)
        )(me, x, y, g, total, side, weights)
        (part,) = call(merge_pair, "vv", [(pairs, K + pairs, LANES)])(keep, sent)
        image = lax.all_to_all(part, chips, 0, 0, tiled=True)
        (mine,) = call(merge_logs, "v", [(pairs, LANES)])(image)
        other = lax.ppermute(mine, "core", swap)

        (image,) = call(merge_chunk, "svv", [(pairs, K, LANES)], cost=work(ns * nt // 2, 2))(me, image, mine)

        tall = (K * ns) // LANES
        target_potential, held = call(
            functools.partial(row_images, math.log2(nt * n_tgt)),
            "svvhvvv",
            [(1, nt), (tall + rows, LANES)],
            [((nt, KD), BF), ((KD, ns), BF), ((80, nt), BF), ((80, ns), F32), ((1, nt), F32), BLOCK, BLOCK],
            cost=work(ns * nt, 2),
        )(me, x, total, image, y, mine, other)
        (image,) = call(hold, "hv", [image.shape], aliases={0: 0}, out="h")(image, held)
        image = lax.all_to_all(image, chips, 0, 0, tiled=True)
        sizes = [held.shape]
        (held,) = call(add, "vv", sizes, cost=work(ns * nt // 4, 2))(held, lax.ppermute(held, tgt, near))
        (held,) = call(add, "vv", sizes, cost=work(ns * nt // 4, 2))(held, lax.ppermute(held, tgt, far))
        source_image, source_potential, target_potential = call(
            add_divide, "vvvv", [(K, ns), (1, ns), (1, nt)], cost=work(ns * nt // 4, 2)
        )(held, lax.ppermute(held, tgt, over), source_potential, target_potential)
        (image,) = call(hold, "vv", [image.shape], aliases={0: 0})(image, held)
        (target_image,) = call(lay_columns, "svv", [(K, nt)])(me, image, lax.ppermute(image, "core", swap))
        return source_potential.reshape(ns), target_potential.reshape(nt), source_image, target_image

    return jax.shard_map(
        shards,
        mesh=grid,
        in_specs=(P(None, src), P(None, tgt), P(tgt)),
        out_specs=(P(src), P(tgt), P(None, src), P(None, tgt)),
        check_vma=False,
    )
```
